768 devices in a mesh: src: 96 (over y_hi, z, core), tgt: 8 (over x, y_lo).
Axes of the slice: x: 4, y: 8 (y_hi: 4, y_lo: 2; y = y_hi * 2 + y_lo), z: 12, core: 2. Of those that a mesh axis runs over, the one named last changes fastest.
Arguments:
- source_items: bfloat16 [49152, 128], P('src'), may hold values from -4 to 4
- target_items: bfloat16 [32768, 128], P('tgt'), may hold values from -4 to 4
- source_mass: float32 [49152], P('src'), may hold values from 0.3 to 4.5
- target_mass: float32 [32768], P('tgt'), may hold values from 0.5 to 2
Outputs:
- mapped: float32 [49152, 128], P('src', 'tgt')
- potential: float32 [32768], P('tgt')
The draws below stay inside these ranges and needn't reach their ends.
All inputs are finite; a program needn't handle non-finite values.
Results may differ from the reference program's by a relative error of at most 0.0014.
Values sent between devices are 32-bit elements; how exact they have to be, the bound alone decides.
A program may use at most 32 MiB of HBM per device.

```python
import math
import jax
import jax.numpy as jnp
from jax import lax

E = 128
SRC_DEV = 512
ITERS = 3
NS = 49152
NT = 32768


def draw_source_mass(key, part):
    key = jax.random.fold_in(key, 11)
    position = jnp.arange(NS, dtype=jnp.float32) / NS
    base = jnp.exp(jax.random.uniform(key, (NS,), jnp.float32, math.log(0.4), math.log(1.2)))
    return base * (1.0 + 2.0 * position)


def shard_levels(rng, shape, split, smallest, high):
    factor_of = 1.0
    for dim, shards_of in split:
        draws = jax.random.uniform(jax.random.fold_in(jax.random.fold_in(rng, 6), dim), (shards_of,), jnp.float32, smallest / len(split), high / len(split))
        factor_of = factor_of * jnp.repeat(jnp.exp(draws), shape[dim] // shards_of).reshape((-1,) + (1,) * (len(shape) - 1 - dim))
    return factor_of


def centred(stream_key, dims, spread, most, pieces=(), kind=jnp.bfloat16):
    gain = shard_levels(stream_key, dims, pieces, -0.22, 0.18) if pieces else 1.0
    drawn = jax.random.normal(stream_key, dims, jnp.float32) * spread * gain
    return jnp.minimum(jnp.maximum(drawn, -most), most).astype(kind)


def setup_inputs(seed: int = 0) -> dict:
    streams_of = jax.random.split(jax.random.key(seed), 5)
    source_items = centred(streams_of[0], (NS, E), 1.0, 4.0, ((0, 96),))
    target_items = centred(streams_of[1], (NT, E), 1.0, 4.0, ((0, 8),))
    source_mass = draw_source_mass(jax.random.fold_in(streams_of[4], 71), 0)
    target_mass = jnp.clip(jnp.exp(math.log(2.0) - 1.3862944 * jax.random.uniform(streams_of[3], (NT,), jnp.float32) ** shard_levels(streams_of[3], (NT,), ((0, 8),), -0.2, 0.2)), 0.5, 2.0)
    return {"source_items": source_items, "target_items": target_items, "source_mass": source_mass, "target_mass": target_mass}


def kernel_of(src_block, target_items):
    logits = jnp.dot(src_block, target_items.T, preferred_element_type=jnp.float32)
    return jnp.exp(logits * (2.0 / math.sqrt(E)))

def sweep(source_items, target_items, row_scale, col_scale):
    blocks = source_items.reshape(NS // SRC_DEV, SRC_DEV, E)
    scales = row_scale.reshape(NS // SRC_DEV, SRC_DEV)

    def visit(carried, inputs):
        src_block, scaled = inputs
        kernel_tile = kernel_of(src_block, target_items)
        row_part = jnp.dot(kernel_tile, col_scale, precision=lax.Precision.HIGHEST)
        carried = carried + jnp.dot(scaled, kernel_tile, precision=lax.Precision.HIGHEST)
        return (carried, row_part)
    col_sums, row_sums = lax.scan(visit, jnp.zeros((NT,), jnp.float32), (blocks, scales))
    return (row_sums.reshape(NS), col_sums)

def reference(source_items, target_items, source_mass, target_mass):
    row_scale = jnp.ones((NS,), jnp.float32)
    col_scale = jnp.ones((NT,), jnp.float32)
    for rounds in range(ITERS):
        row_sums, col_sums = sweep(source_items, target_items, row_scale, col_scale)
        fresh_row = source_mass / row_sums
        col_scale = target_mass / col_sums
        row_scale = fresh_row
    blocks = source_items.reshape(NS // SRC_DEV, SRC_DEV, E)
    unit_column = jnp.ones((NT,), jnp.bfloat16)

    def image(src_block):
        kernel_tile = kernel_of(src_block, target_items)
        weights = (kernel_tile * col_scale[None, :]).astype(jnp.bfloat16)
        numerator = jnp.dot(weights, target_items, preferred_element_type=jnp.float32)
        denominator = jnp.dot(weights, unit_column, preferred_element_type=jnp.float32)
        return numerator / denominator[:, None]
    mapped = lax.map(image, blocks).reshape(NS, E)
    potential = jnp.log(NS * col_scale)
    return (mapped, potential)
```

```python
import functools
import math

import jax
import jax.numpy as jnp
from jax import lax
from jax.experimental import pallas as pl
from jax.experimental.pallas import tpu as pltpu
from jax.sharding import PartitionSpec as P

ROWS = 512
COLS = 4096
EMBED = 128
DEPTH = 12
PAIR = 2
TEAM = 8
PART = COLS // TEAM
TGT = 8
SLIVER = EMBED // TGT
MESH = pl.DeviceIdType.MESH
F32 = jnp.float32
BF16 = jnp.bfloat16


def kernel(
    source_count,
    s_hbm, t_hbm, rmass_hbm, cmass_hbm,
    map_ref, pot_ref,
    s_v, text, rmass, cmass, kmat,
    col_send, col_recv, z_buf, c_buf,
    row_acc, row_buf, row_wide,
    num, num_t, num_recv, den_t, den_recv,
    load_sem, team_send, team_recv, z_send, z_recv, c_send, c_recv,
    row_send, row_recv, num_send, num_rsem, den_send, den_rsem,
):
    me_s, me_t = lax.axis_index("src"), lax.axis_index("tgt")
    core = lax.rem(me_s, PAIR)
    chip = lax.div(me_s, PAIR)
    zed = lax.rem(chip, DEPTH)
    member = lax.div(chip, DEPTH) * PAIR + core

    def mate(k):
        other = lax.rem(member + k, TEAM)
        return (
            (lax.div(other, PAIR) * DEPTH + zed) * PAIR + lax.rem(other, PAIR),
            me_t,
        )

    def level(k):
        return (
            (lax.div(member, PAIR) * DEPTH + lax.rem(zed + k, DEPTH)) * PAIR + core,
            me_t,
        )

    def across(k):
        return (me_s, lax.rem(me_t + k, TGT))

    loads = [
        pltpu.make_async_copy(s_hbm, s_v, load_sem.at[0]),
        pltpu.make_async_copy(t_hbm, text.at[:, :, pl.ds(0, EMBED)], load_sem.at[1]),
        pltpu.make_async_copy(rmass_hbm, rmass, load_sem.at[2]),
        pltpu.make_async_copy(cmass_hbm, cmass, load_sem.at[3]),
    ]
    for load in loads:
        load.start()

    barrier = pltpu.get_barrier_semaphore()
    friends = (
        [mate(k) for k in range(1, TEAM)]
        + [level(k) for k in range(1, DEPTH)]
        + [across(k) for k in range(1, TGT)]
    )
    for friend in friends:
        pl.semaphore_signal(barrier, inc=1, device_id=friend, device_id_type=MESH)

    text[:, :, pl.ds(EMBED, EMBED)] = jnp.ones((TEAM, PART, EMBED), BF16)
    loads[0].wait()
    loads[1].wait()

    def remote(src, dst, send, recv, where):
        return pltpu.make_async_remote_copy(
            src_ref=src, dst_ref=dst, send_sem=send, recv_sem=recv,
            device_id=where, device_id_type=MESH,
        )

    def spread_columns(it, part_of):
        for k in range(1, TEAM + 1):
            q = lax.rem(member + k, TEAM)
            col_send[it, k - 1] = part_of(q)
            if k < TEAM:
                if it == 0 and k == 1:
                    pl.semaphore_wait(barrier, len(friends))
                remote(
                    col_send.at[it, k - 1], col_recv.at[it, k - 1],
                    team_send.at[it], team_recv.at[it], mate(k),
                ).start()
        everyone = pl.ds(0, TEAM - 1)
        team = remote(
            col_send.at[it, everyone], col_recv.at[it, everyone],
            team_send.at[it], team_recv.at[it], mate(1),
        )
        team.wait_recv()
        total = col_send[it, TEAM - 1]
        for k in range(TEAM - 1):
            total = total + col_recv[it, k]
        z_buf[it, zed] = total
        for k in range(1, DEPTH):
            remote(
                z_buf.at[it, zed], z_buf.at[it, zed],
                z_send.at[it], z_recv.at[it], level(k),
            ).start()
        team.wait_send()
        others = pl.ds(0, DEPTH - 1)
        floor = remote(
            z_buf.at[it, others], z_buf.at[it, others],
            z_send.at[it], z_recv.at[it], level(1),
        )
        if it == 0:
            loads[3].wait()
        floor.wait_recv()
        total = z_buf[it, 0]
        for k in range(1, DEPTH):
            total = total + z_buf[it, k]
        c_buf[it, member] = cmass[member] / total
        copies = [
            remote(
                c_buf.at[it, member], c_buf.at[it, member],
                c_send.at[it], c_recv.at[it, k], mate(k),
            )
            for k in range(1, TEAM)
        ]
        for copy in copies:
            copy.start()
        floor.wait_send()

        def arrival(k):
            if k:
                copies[k - 1].wait_recv()
            return lax.rem(member + TEAM - k, TEAM)

        def flush():
            remote(
                c_buf.at[it, everyone], c_buf.at[it, everyone],
                c_send.at[it], c_recv.at[it, 1], mate(1),
            ).wait_send()

        return arrival, flush

    log2e = 1.4426950408889634
    factor = 2.0 / math.sqrt(EMBED) * log2e

    def first_part(q):
        pieces = []
        for h in range(PART // 256):
            cols = pl.ds(h * 256, 256)
            logits = lax.dot_general(
                s_v[...], text[q, cols, pl.ds(0, EMBED)],
                (((1,), (1,)), ((), ())), preferred_element_type=F32,
            )
            tile = jnp.exp2(logits * factor)
            kmat[q, :, cols] = tile
            pieces.append(jnp.sum(tile, axis=0, keepdims=True))
        return jnp.concatenate(pieces, axis=1)

    arrival, flush = spread_columns(0, first_part)
    loads[2].wait()

    for k in range(TEAM):
        q = arrival(k)
        scale = c_buf[0, q]
        fold = None
        for lane in range(PART // 128):
            cols = pl.ds(lane * 128, 128)
            term = kmat[q, :, cols] * scale[:, lane * 128 : lane * 128 + 128]
            fold = term if fold is None else fold + term
        if k == 0:
            row_acc[...] = fold
        else:
            row_acc[...] += fold
    row_buf[me_t] = jnp.sum(row_acc[...].T, axis=0, keepdims=True)
    for k in range(1, TGT):
        remote(
            row_buf.at[me_t], row_buf.at[me_t], row_send, row_recv, across(k)
        ).start()
    flush()
    rest = pl.ds(0, TGT - 1)
    rows = remote(row_buf.at[rest], row_buf.at[rest], row_send, row_recv, across(1))
    rows.wait_recv()
    total = row_buf[0]
    for k in range(1, TGT):
        total = total + row_buf[k]
    row_wide[...] = jnp.broadcast_to(rmass[...] / total, (128, ROWS)).T

    def second_part(q):
        pieces = []
        for lane in range(PART // 128):
            cols = pl.ds(lane * 128, 128)
            pieces.append(
                jnp.sum(kmat[q, :, cols] * row_wide[...], axis=0, keepdims=True)
            )
        return jnp.concatenate(pieces, axis=1)

    arrival, flush = spread_columns(1, second_part)
    rows.wait_send()

    half = ROWS // 2
    for k in range(TEAM):
        q = arrival(k)
        scale = c_buf[1, q]
        if k < TEAM - 1:
            weights = (kmat[q] * scale).astype(BF16)
            term = jnp.dot(weights, text[q], preferred_element_type=F32)
            if k == 0:
                num[...] = term
            else:
                num[...] += term
            continue
        for h in range(2):
            span = pl.ds(h * half, half)
            weights = (kmat[q, span, :] * scale).astype(BF16)
            term = jnp.dot(weights, text[q], preferred_element_type=F32)
            term = term + num[span, :]
            num_t[:, :, span] = term[:, :EMBED].T.reshape(TGT, SLIVER, half)
            den_t[:, span] = term[:, EMBED:].T[:1]
            for j in range(1, TGT):
                there = lax.rem(me_t + j, TGT)
                remote(
                    num_t.at[there, :, span], num_recv.at[j - 1, :, span],
                    num_send.at[h], num_rsem.at[h], across(j),
                ).start()
                remote(
                    den_t.at[:, span], den_recv.at[j - 1, :, span],
                    den_send.at[h], den_rsem.at[h], across(j),
                ).start()
    flush()
    pot_ref[...] = jnp.log(source_count * c_buf[1])
    last = []
    for h in range(2):
        span = pl.ds(h * half, half)
        num_copy = remote(
            num_t.at[rest, :, span], num_recv.at[:, :, span],
            num_send.at[h], num_rsem.at[h], across(1),
        )
        den_copy = remote(
            den_recv.at[:, :, span], den_recv.at[:, :, span],
            den_send.at[h], den_rsem.at[h], across(1),
        )
        den_copy.wait_recv()
        den_total = den_t[:, span]
        for j in range(TGT - 1):
            den_total = den_total + den_recv[j, :, span]
        num_copy.wait_recv()
        num_total = num_t[me_t, :, span]
        for j in range(TGT - 1):
            num_total = num_total + num_recv[j, :, span]
        map_ref[:, span] = num_total / den_total
        last += [num_copy, den_copy]
    for copy in last:
        copy.wait_send()


def on_device(source_items, target_items, source_mass, target_mass):
    source_count = source_items.shape[0] * lax.axis_size("src")
    any_spec = pl.BlockSpec(memory_space=pl.ANY)
    vmem_spec = pl.BlockSpec(memory_space=pltpu.VMEM)
    vmem, dma = pltpu.VMEM, pltpu.SemaphoreType.DMA
    mapped, potential = pl.pallas_call(
        functools.partial(kernel, float(source_count)),
        out_shape=(
            jax.ShapeDtypeStruct((SLIVER, ROWS), F32),
            jax.ShapeDtypeStruct((TEAM, 1, PART), F32),
        ),
        in_specs=[any_spec] * 4,
        out_specs=(vmem_spec, vmem_spec),
        scratch_shapes=[
            vmem((ROWS, EMBED), BF16),
            vmem((TEAM, PART, 2 * EMBED), BF16),
            vmem((1, ROWS), F32),
            vmem((TEAM, 1, PART), F32),
            vmem((TEAM, ROWS, PART), F32),
            vmem((2, TEAM, 1, PART), F32),
            vmem((2, TEAM - 1, 1, PART), F32),
            vmem((2, DEPTH, 1, PART), F32),
            vmem((2, TEAM, 1, PART), F32),
            vmem((ROWS, 128), F32),
            vmem((TGT, 1, ROWS), F32),
            vmem((ROWS, 128), F32),
            vmem((ROWS, 2 * EMBED), F32),
            vmem((TGT, SLIVER, ROWS), F32),
            vmem((TGT - 1, SLIVER, ROWS), F32),
            vmem((1, ROWS), F32),
            vmem((TGT - 1, 1, ROWS), F32),
            dma((4,)),
            dma((2,)),
            dma((2,)),
            dma((2,)),
            dma((2,)),
            dma((2,)),
            dma((2, TEAM)),
            dma,
            dma,
            dma((2,)),
            dma((2,)),
            dma((2,)),
            dma((2,)),
        ],
        compiler_params=pltpu.CompilerParams(
            collective_id=0,
            has_side_effects=True,
            vmem_limit_bytes=40 * 1024 * 1024,
        ),
    )(
        source_items,
        target_items.reshape(TEAM, PART, EMBED),
        source_mass.reshape(1, ROWS),
        target_mass.reshape(TEAM, 1, PART),
    )
    return mapped.T, potential.reshape(COLS)


def solution(mesh):
    in_specs = (P("src", None), P("tgt", None), P("src"), P("tgt"))
    out_specs = (P("src", "tgt"), P("tgt"))
    return jax.shard_map(
        on_device, mesh=mesh, in_specs=in_specs, out_specs=out_specs, check_vma=False
    )
```

```python
import functools
import math

import jax
import jax.numpy as jnp
from jax import lax
from jax.experimental import pallas as pl
from jax.experimental.pallas import tpu as pltpu
from jax.sharding import PartitionSpec as P

ROWS = 512
COLS = 4096
EMBED = 128
RING = 4
DEPTH = 12
PAIR = 2
HALF = COLS // PAIR
LANES = 128
TILES = HALF // LANES
TGT = 8
SLIVER = EMBED // TGT
SPAN = 256
MESH = pl.DeviceIdType.MESH
F32 = jnp.float32
BF16 = jnp.bfloat16
RING_STEPS = (2, 1, 3)
DEPTH_STEPS = (6, 5, 7, 4, 8, 3, 9, 2, 10, 1, 11)
TGT_STEPS = ((2, 1), (2, 0), (1, 1), (3, 1), (1, 0), (3, 0), (0, 1))


def kernel(
    source_count,
    s_hbm, t_hbm, rmass_hbm, cmass_hbm,
    map_ref, pot_ref,
    s_v, text, rmass, cmass, kmat,
    part, half_out, half_in, y_buf, z_buf, c_buf,
    row_acc, row_buf, row_scale, row_wide,
    num, num_t, num_recv, den_t, den_recv,
    load_sem, enter_sem, half_send, half_recv, y_send, y_recv, z_send, z_recv,
    c_send, c_recv, row_send, row_recv, num_send, num_rsem, den_send, den_rsem,
):
    me_s, me_t = lax.axis_index("src"), lax.axis_index("tgt")
    core = lax.rem(me_s, PAIR)
    chip = lax.div(me_s, PAIR)
    zed = lax.rem(chip, DEPTH)
    ring = lax.div(chip, DEPTH)
    twin = 1 - core
    place_x, place_y = lax.div(me_t, 2), lax.rem(me_t, 2)

    def source(ring_at, zed_at, core_at):
        return (ring_at * DEPTH + zed_at) * PAIR + core_at

    twin_id = (source(ring, zed, twin), me_t)
    ring_ids = [(source(lax.rem(ring + k, RING), zed, core), me_t) for k in RING_STEPS]
    depth_at = [lax.rem(zed + k, DEPTH) for k in DEPTH_STEPS]
    depth_ids = [(source(ring, there, core), me_t) for there in depth_at]
    tgt_at = [
        lax.rem(place_x + dx, 4) * 2 + lax.rem(place_y + dy, 2) for dx, dy in TGT_STEPS
    ]
    same_ids = [(me_s, there) for there in tgt_at]

    quarter = HALF // 2
    loads = [pltpu.make_async_copy(s_hbm, s_v, load_sem.at[0])]
    for i, (side, owner) in enumerate(((1, twin), (1, twin), (0, core), (0, core))):
        span = pl.ds(i % 2 * quarter, quarter)
        loads.append(
            pltpu.make_async_copy(
                t_hbm.at[owner, span, :],
                text.at[side, span, pl.ds(0, EMBED)],
                load_sem.at[i + 1],
            )
        )
    loads += [
        pltpu.make_async_copy(rmass_hbm, rmass, load_sem.at[5]),
        pltpu.make_async_copy(cmass_hbm.at[core], cmass, load_sem.at[6]),
    ]
    for load in loads:
        load.start()

    barrier = pltpu.get_barrier_semaphore()
    friends = ring_ids + same_ids + [twin_id]
    for friend in friends:
        pl.semaphore_signal(barrier, inc=1, device_id=friend, device_id_type=MESH)
    for there, friend in zip(depth_at, depth_ids):

        @pl.when(there > zed)
        def _():
            pl.semaphore_signal(barrier, inc=1, device_id=friend, device_id_type=MESH)

    def remote(src, dst, send, recv, where):
        return pltpu.make_async_remote_copy(
            src_ref=src, dst_ref=dst, send_sem=send, recv_sem=recv,
            device_id=where, device_id_type=MESH,
        )

    log2e = 1.4426950408889634
    factor = 2.0 / math.sqrt(EMBED) * log2e
    block = 256

    def kernel_piece(side, piece, sums_ref):
        sums = None
        for m in range(ROWS // block):
            logits = lax.dot_general(
                s_v[pl.ds(m * block, block), :],
                text[side, pl.ds(piece * 256, 256), pl.ds(0, EMBED)],
                (((1,), (1,)), ((), ())), preferred_element_type=F32,
            )
            tile = jnp.exp2(logits * factor)
            for i in range(2):
                kmat[side, piece * 2 + i, pl.ds(m * block, block), :] = tile[
                    :, i * LANES : (i + 1) * LANES
                ]
            term = jnp.sum(tile.reshape(block // 8, 8, 256), axis=0)
            sums = term if sums is None else sums + term
        sums = jnp.sum(sums, axis=0, keepdims=True)
        for i in range(2):
            sums_ref[pl.ds(piece * 2 + i, 1), :] = sums[:, i * LANES : (i + 1) * LANES]

    def half_copy(it):
        return remote(
            half_out.at[it], half_in.at[it], half_send.at[it], half_recv.at[it], twin_id
        )

    loads[0].wait()
    pieces = HALF // 256
    for piece in range(pieces):
        if piece % (pieces // 2) == 0:
            loads[1 + piece // (pieces // 2)].wait()
        kernel_piece(1, piece, half_out.at[0])
    for piece in range(pieces):
        if piece % (pieces // 2) == 0:
            loads[3 + piece // (pieces // 2)].wait()
        if piece == pieces // 2:
            pl.semaphore_wait(barrier, len(friends) + zed)
            half_copy(0).start()
            for there, friend in zip(depth_at, depth_ids):

                @pl.when(there < zed)
                def _():
                    pl.semaphore_signal(
                        enter_sem, inc=1, device_id=friend, device_id_type=MESH
                    )

        kernel_piece(0, piece, part)

    def finish_columns(it, meanwhile):
        half_copy(it).wait_recv()
        y_buf[it, ring] = part[...] + half_in[it]
        for where in ring_ids:
            remote(
                y_buf.at[it, ring], y_buf.at[it, ring], y_send.at[it], y_recv.at[it], where
            ).start()
        half_copy(it).wait_send()
        meanwhile()
        others = pl.ds(0, RING - 1)
        trio = remote(
            y_buf.at[it, others], y_buf.at[it, others],
            y_send.at[it], y_recv.at[it], twin_id,
        )
        trio.wait_recv()
        total = y_buf[it, 0]
        for k in range(1, RING):
            total = total + y_buf[it, k]
        z_buf[it, zed] = total

        def send_depth(where):
            remote(
                z_buf.at[it, zed], z_buf.at[it, zed], z_send.at[it], z_recv.at[it], where
            ).start()

        if it == 0:
            for there, where in zip(depth_at, depth_ids):

                @pl.when(there < zed)
                def _():
                    send_depth(where)

            @pl.when(zed < DEPTH - 1)
            def _():
                pl.semaphore_wait(enter_sem, DEPTH - 1 - zed)

            for there, where in zip(depth_at, depth_ids):

                @pl.when(there > zed)
                def _():
                    send_depth(where)

        else:
            for where in depth_ids:
                send_depth(where)
        trio.wait_send()
        others = pl.ds(0, DEPTH - 1)
        column = remote(
            z_buf.at[it, others], z_buf.at[it, others],
            z_send.at[it], z_recv.at[it], twin_id,
        )
        column.wait_recv()
        total = z_buf[it, 0]
        for k in range(1, DEPTH):
            total = total + z_buf[it, k]
        c_buf[it, 0] = cmass[...] / total
        mirror = remote(
            c_buf.at[it, 0], c_buf.at[it, 1], c_send.at[it], c_recv.at[it], twin_id
        )
        mirror.start()
        return column, mirror

    def first_wait():
        text[:, :, pl.ds(EMBED, EMBED)] = jnp.ones((PAIR, HALF, EMBED), BF16)
        for load in loads[5:]:
            load.wait()

    column, mirror = finish_columns(0, first_wait)

    step = 64
    for side in range(PAIR):
        if side == 1:
            column.wait_send()
            mirror.wait_recv()
        for b in range(ROWS // step):
            span = pl.ds(b * step, step)
            fold = kmat[side, 0, span, :] * c_buf[0, side, pl.ds(0, 1), :]
            for r in range(1, TILES):
                fold = fold + kmat[side, r, span, :] * c_buf[0, side, pl.ds(r, 1), :]
            if side == 1:
                fold = fold + row_acc[span, :]
            row_acc[span, :] = fold
    for i in range(ROWS // LANES):
        row_buf[me_t, pl.ds(i, 1), :] = jnp.sum(
            row_acc[pl.ds(i * LANES, LANES), :].T, axis=0, keepdims=True
        )
    for where in same_ids:
        remote(
            row_buf.at[me_t], row_buf.at[me_t], row_send, row_recv, where
        ).start()
    mirror.wait_send()
    rest = pl.ds(0, TGT - 1)
    rows = remote(row_buf.at[rest], row_buf.at[rest], row_send, row_recv, twin_id)
    rows.wait_recv()
    total = row_buf[0]
    for k in range(1, TGT):
        total = total + row_buf[k]
    row_scale[...] = rmass[...] / total
    for i in range(ROWS // LANES):
        wide = jnp.broadcast_to(row_scale[pl.ds(i, 1), :], (LANES, LANES))
        row_wide[pl.ds(i * LANES, LANES), :] = wide.T

    for side, sums_ref in ((1, half_out.at[1]), (0, part)):
        sums = [jnp.zeros((8, LANES), F32)] * TILES
        for b in range(ROWS // step):
            span = pl.ds(b * step, step)
            wide = row_wide[span, :]
            for r in range(TILES):
                term = (kmat[side, r, span, :] * wide).reshape(step // 8, 8, LANES)
                sums[r] = sums[r] + jnp.sum(term, axis=0)
        for r in range(TILES):
            sums_ref[pl.ds(r, 1), :] = jnp.sum(sums[r], axis=0, keepdims=True)
        if side == 1:
            half_copy(1).start()

    column, mirror = finish_columns(1, rows.wait_send)

    def weighted(side, span):
        weights = jnp.concatenate(
            [
                (kmat[side, r, span, :] * c_buf[1, side, pl.ds(r, 1), :]).astype(BF16)
                for r in range(TILES)
            ],
            axis=1,
        )
        return jnp.dot(weights, text[side], preferred_element_type=F32)

    for h in range(ROWS // SPAN):
        span = pl.ds(h * SPAN, SPAN)
        num[span, :] = weighted(0, span)
    mirror.wait_recv()
    for h in range(ROWS // SPAN):
        span = pl.ds(h * SPAN, SPAN)
        term = weighted(1, span) + num[span, :]
        num_t[:, :, span] = term[:, :EMBED].T.reshape(TGT, SLIVER, SPAN)
        den_t[:, span] = term[:, EMBED:].T[:1]
        for j, there in enumerate(tgt_at):
            remote(
                num_t.at[there, :, span], num_recv.at[j, :, span],
                num_send.at[h], num_rsem.at[h], same_ids[j],
            ).start()
    for j in range(TGT - 1):
        remote(den_t, den_recv.at[j], den_send, den_rsem, same_ids[j]).start()

    pot_ref[core] = jnp.log(source_count * c_buf[1, 0])
    pot_ref[twin] = jnp.log(source_count * c_buf[1, 1])
    column.wait_send()
    mirror.wait_send()
    last = []
    for h in range(ROWS // SPAN):
        span = pl.ds(h * SPAN, SPAN)
        last.append(
            remote(
                num_t.at[pl.ds(0, TGT - 1), :, span], num_recv.at[:, :, span],
                num_send.at[h], num_rsem.at[h], twin_id,
            )
        )
    den_copy = remote(den_recv, den_recv, den_send, den_rsem, twin_id)
    den_copy.wait_recv()
    den_total = den_t[...]
    for j in range(TGT - 1):
        den_total = den_total + den_recv[j]
    for h in range(ROWS // SPAN):
        span = pl.ds(h * SPAN, SPAN)
        last[h].wait_recv()
        num_total = num_t[me_t, :, span]
        for j in range(TGT - 1):
            num_total = num_total + num_recv[j, :, span]
        map_ref[:, span] = num_total / den_total[:, h * SPAN : (h + 1) * SPAN]
    for copy in last + [den_copy]:
        copy.wait_send()


def on_device(source_items, target_items, source_mass, target_mass):
    source_count = source_items.shape[0] * lax.axis_size("src")
    any_spec = pl.BlockSpec(memory_space=pltpu.HBM)
    vmem_spec = pl.BlockSpec(memory_space=pltpu.VMEM)
    vmem, dma = pltpu.VMEM, pltpu.SemaphoreType.DMA
    mapped, potential = pl.pallas_call(
        functools.partial(kernel, float(source_count)),
        out_shape=(
            jax.ShapeDtypeStruct((SLIVER, ROWS), F32),
            jax.ShapeDtypeStruct((PAIR, TILES, LANES), F32),
        ),
        in_specs=[any_spec] * 4,
        out_specs=(vmem_spec, vmem_spec),
        scratch_shapes=[
            vmem((ROWS, EMBED), BF16),
            vmem((PAIR, HALF, 2 * EMBED), BF16),
            vmem((ROWS // LANES, LANES), F32),
            vmem((TILES, LANES), F32),
            vmem((PAIR, TILES, ROWS, LANES), F32),
            vmem((TILES, LANES), F32),
            vmem((2, TILES, LANES), F32),
            vmem((2, TILES, LANES), F32),
            vmem((2, RING, TILES, LANES), F32),
            vmem((2, DEPTH, TILES, LANES), F32),
            vmem((2, PAIR, TILES, LANES), F32),
            vmem((ROWS, LANES), F32),
            vmem((TGT, ROWS // LANES, LANES), F32),
            vmem((ROWS // LANES, LANES), F32),
            vmem((ROWS, LANES), F32),
            vmem((ROWS, 2 * EMBED), F32),
            vmem((TGT, SLIVER, ROWS), F32),
            vmem((TGT - 1, SLIVER, ROWS), F32),
            vmem((1, ROWS), F32),
            vmem((TGT - 1, 1, ROWS), F32),
            dma((7,)),
            pltpu.SemaphoreType.REGULAR,
            dma((2,)),
            dma((2,)),
            dma((2,)),
            dma((2,)),
            dma((2,)),
            dma((2,)),
            dma((2,)),
            dma((2,)),
            dma,
            dma,
            dma((ROWS // SPAN,)),
            dma((ROWS // SPAN,)),
            dma,
            dma,
        ],
        compiler_params=pltpu.CompilerParams(
            collective_id=0,
            has_side_effects=True,
            vmem_limit_bytes=56000 * 1024,
        ),
    )(
        source_items,
        target_items.reshape(PAIR, HALF, EMBED),
        source_mass.reshape(ROWS // LANES, LANES),
        target_mass.reshape(PAIR, TILES, LANES),
    )
    return mapped.T, potential.reshape(COLS)


def solution(mesh):
    in_specs = (P("src", None), P("tgt", None), P("src"), P("tgt"))
    out_specs = (P("src", "tgt"), P("tgt"))
    return jax.shard_map(
        on_device, mesh=mesh, in_specs=in_specs, out_specs=out_specs, check_vma=False
    )
```

```python
import functools
import math

import jax
import jax.numpy as jnp
from jax import lax
from jax.experimental import pallas as pl
from jax.experimental.pallas import tpu as pltpu
from jax.sharding import PartitionSpec as P

ROWS = 512
COLS = 4096
EMBED = 128
RING = 4
DEPTH = 12
PAIR = 2
HALF = COLS // PAIR
LANES = 128
TILES = HALF // LANES
TGT = 8
SLIVER = EMBED // TGT
SPAN = 256
LIMIT = 40 * 1024
MESH = pl.DeviceIdType.MESH
F32 = jnp.float32
BF16 = jnp.bfloat16
RING_STEPS = (2, 1, 3)
DEPTH_STEPS = (6, 5, 7, 4, 8, 3, 9, 2, 10, 1, 11)
TGT_STEPS = ((2, 1), (2, 0), (1, 1), (3, 1), (1, 0), (3, 0), (0, 1))


def kernel(
    source_count,
    s_hbm, t_hbm, rmass_hbm, cmass_hbm,
    map_ref, pot_ref,
    s_v, text, rmass, cmass, kmat,
    part, half_out, half_in, y_buf, z_buf, c_buf,
    row_acc, row_buf, row_scale, row_wide,
    num, num_t, num_recv, den_t, den_recv,
    load_sem, enter_sem, half_send, half_recv, y_send, y_recv, z_send, z_recv,
    c_send, c_recv, row_send, row_recv, num_send, num_rsem, den_send, den_rsem,
):
    me_s, me_t = lax.axis_index("src"), lax.axis_index("tgt")
    core = lax.rem(me_s, PAIR)
    chip = lax.div(me_s, PAIR)
    zed = lax.rem(chip, DEPTH)
    ring = lax.div(chip, DEPTH)
    twin = 1 - core
    place_x, place_y = lax.div(me_t, 2), lax.rem(me_t, 2)

    def source(ring_at, zed_at, core_at):
        return (ring_at * DEPTH + zed_at) * PAIR + core_at

    twin_id = (source(ring, zed, twin), me_t)
    ring_ids = [(source(lax.rem(ring + k, RING), zed, core), me_t) for k in RING_STEPS]
    depth_at = [lax.rem(zed + k, DEPTH) for k in DEPTH_STEPS]
    depth_ids = [(source(ring, there, core), me_t) for there in depth_at]
    tgt_at = [
        lax.rem(place_x + dx, 4) * 2 + lax.rem(place_y + dy, 2) for dx, dy in TGT_STEPS
    ]
    same_ids = [(me_s, there) for there in tgt_at]

    quarter = HALF // 2
    loads = [pltpu.make_async_copy(s_hbm, s_v, load_sem.at[0])]
    for i, (side, owner) in enumerate(((1, twin), (1, twin), (0, core), (0, core))):
        span = pl.ds(i % 2 * quarter, quarter)
        loads.append(
            pltpu.make_async_copy(
                t_hbm.at[owner, span, :],
                text.at[side, span, pl.ds(0, EMBED)],
                load_sem.at[i + 1],
            )
        )
    loads += [
        pltpu.make_async_copy(rmass_hbm, rmass, load_sem.at[5]),
        pltpu.make_async_copy(cmass_hbm.at[core], cmass, load_sem.at[6]),
    ]
    for load in loads:
        load.start()

    barrier = pltpu.get_barrier_semaphore()
    friends = ring_ids + same_ids + [twin_id]
    for friend in friends:
        pl.semaphore_signal(barrier, inc=1, device_id=friend, device_id_type=MESH)
    for there, friend in zip(depth_at, depth_ids):

        @pl.when(there > zed)
        def _():
            pl.semaphore_signal(barrier, inc=1, device_id=friend, device_id_type=MESH)

    def remote(src, dst, send, recv, where):
        return pltpu.make_async_remote_copy(
            src_ref=src, dst_ref=dst, send_sem=send, recv_sem=recv,
            device_id=where, device_id_type=MESH,
        )

    log2e = 1.4426950408889634
    factor = 2.0 / math.sqrt(EMBED) * log2e
    block = 256

    def kernel_piece(side, piece, sums_ref):
        sums = None
        for m in range(ROWS // block):
            logits = lax.dot_general(
                s_v[pl.ds(m * block, block), :],
                text[side, pl.ds(piece * 256, 256), pl.ds(0, EMBED)],
                (((1,), (1,)), ((), ())), preferred_element_type=F32,
            )
            tile = jnp.exp2(logits * factor)
            for i in range(2):
                kmat[side, piece * 2 + i, pl.ds(m * block, block), :] = tile[
                    :, i * LANES : (i + 1) * LANES
                ]
            term = jnp.sum(tile.reshape(block // 8, 8, 256), axis=0)
            sums = term if sums is None else sums + term
        sums = jnp.sum(sums, axis=0, keepdims=True)
        for i in range(2):
            sums_ref[pl.ds(piece * 2 + i, 1), :] = sums[:, i * LANES : (i + 1) * LANES]

    def half_copy(it):
        return remote(
            half_out.at[it], half_in.at[it], half_send.at[it], half_recv.at[it], twin_id
        )

    loads[0].wait()
    pieces = HALF // 256
    for piece in range(pieces):
        if piece % (pieces // 2) == 0:
            loads[1 + piece // (pieces // 2)].wait()
        kernel_piece(1, piece, half_out.at[0])
    for piece in range(pieces):
        if piece % (pieces // 2) == 0:
            loads[3 + piece // (pieces // 2)].wait()
        if piece == pieces // 2:
            pl.semaphore_wait(barrier, len(friends) + zed)
            half_copy(0).start()
            for there, friend in zip(depth_at, depth_ids):

                @pl.when(there < zed)
                def _():
                    pl.semaphore_signal(
                        enter_sem, inc=1, device_id=friend, device_id_type=MESH
                    )

        kernel_piece(0, piece, part)

    def finish_columns(it, meanwhile):
        half_copy(it).wait_recv()
        y_buf[it, ring] = part[...] + half_in[it]
        for where in ring_ids:
            remote(
                y_buf.at[it, ring], y_buf.at[it, ring], y_send.at[it], y_recv.at[it], where
            ).start()
        half_copy(it).wait_send()
        meanwhile()
        others = pl.ds(0, RING - 1)
        trio = remote(
            y_buf.at[it, others], y_buf.at[it, others],
            y_send.at[it], y_recv.at[it], twin_id,
        )
        trio.wait_recv()
        total = y_buf[it, 0]
        for k in range(1, RING):
            total = total + y_buf[it, k]
        z_buf[it, zed] = total

        def send_depth(where):
            remote(
                z_buf.at[it, zed], z_buf.at[it, zed], z_send.at[it], z_recv.at[it], where
            ).start()

        if it == 0:
            for there, where in zip(depth_at, depth_ids):

                @pl.when(there < zed)
                def _():
                    send_depth(where)

            @pl.when(zed < DEPTH - 1)
            def _():
                pl.semaphore_wait(enter_sem, DEPTH - 1 - zed)

            for there, where in zip(depth_at, depth_ids):

                @pl.when(there > zed)
                def _():
                    send_depth(where)

        else:
            for where in depth_ids:
                send_depth(where)
        trio.wait_send()
        others = pl.ds(0, DEPTH - 1)
        column = remote(
            z_buf.at[it, others], z_buf.at[it, others],
            z_send.at[it], z_recv.at[it], twin_id,
        )
        column.wait_recv()
        total = z_buf[it, 0]
        for k in range(1, DEPTH):
            total = total + z_buf[it, k]
        c_buf[it, 0] = cmass[...] / total
        mirror = remote(
            c_buf.at[it, 0], c_buf.at[it, 1], c_send.at[it], c_recv.at[it], twin_id
        )
        mirror.start()
        return column, mirror

    def first_wait():
        text[:, :, pl.ds(EMBED, EMBED)] = jnp.ones((PAIR, HALF, EMBED), BF16)
        for load in loads[5:]:
            load.wait()

    column, mirror = finish_columns(0, first_wait)

    step = 64
    for side in range(PAIR):
        if side == 1:
            column.wait_send()
            mirror.wait_recv()
        for b in range(ROWS // step):
            span = pl.ds(b * step, step)
            fold = kmat[side, 0, span, :] * c_buf[0, side, pl.ds(0, 1), :]
            for r in range(1, TILES):
                fold = fold + kmat[side, r, span, :] * c_buf[0, side, pl.ds(r, 1), :]
            if side == 1:
                fold = fold + row_acc[span, :]
            row_acc[span, :] = fold
    for i in range(ROWS // LANES):
        row_buf[me_t, pl.ds(i, 1), :] = jnp.sum(
            row_acc[pl.ds(i * LANES, LANES), :].T, axis=0, keepdims=True
        )
    for where in same_ids:
        remote(
            row_buf.at[me_t], row_buf.at[me_t], row_send, row_recv, where
        ).start()
    mirror.wait_send()
    rest = pl.ds(0, TGT - 1)
    rows = remote(row_buf.at[rest], row_buf.at[rest], row_send, row_recv, twin_id)
    rows.wait_recv()
    total = row_buf[0]
    for k in range(1, TGT):
        total = total + row_buf[k]
    row_scale[...] = rmass[...] / total
    for i in range(ROWS // LANES):
        wide = jnp.broadcast_to(row_scale[pl.ds(i, 1), :], (LANES, LANES))
        row_wide[pl.ds(i * LANES, LANES), :] = wide.T

    for side, sums_ref in ((1, half_out.at[1]), (0, part)):
        sums = [jnp.zeros((8, LANES), F32)] * TILES
        for b in range(ROWS // step):
            span = pl.ds(b * step, step)
            wide = row_wide[span, :]
            for r in range(TILES):
                term = (kmat[side, r, span, :] * wide).reshape(step // 8, 8, LANES)
                sums[r] = sums[r] + jnp.sum(term, axis=0)
        for r in range(TILES):
            sums_ref[pl.ds(r, 1), :] = jnp.sum(sums[r], axis=0, keepdims=True)
        if side == 1:
            half_copy(1).start()

    column, mirror = finish_columns(1, rows.wait_send)

    def weighted(side, span):
        weights = jnp.concatenate(
            [
                (kmat[side, r, span, :] * c_buf[1, side, pl.ds(r, 1), :]).astype(BF16)
                for r in range(TILES)
            ],
            axis=1,
        )
        return jnp.dot(weights, text[side], preferred_element_type=F32)

    for h in range(ROWS // SPAN):
        span = pl.ds(h * SPAN, SPAN)
        num[span, :] = weighted(0, span)
    mirror.wait_recv()
    for h in range(ROWS // SPAN):
        span = pl.ds(h * SPAN, SPAN)
        term = weighted(1, span) + num[span, :]
        num_t[:, :, span] = term[:, :EMBED].T.reshape(TGT, SLIVER, SPAN)
        den_t[:, span] = term[:, EMBED:].T[:1]
        for j, there in enumerate(tgt_at):
            remote(
                num_t.at[there, :, span], num_recv.at[j, :, span],
                num_send.at[h], num_rsem.at[h], same_ids[j],
            ).start()
    for j in range(TGT - 1):
        remote(den_t, den_recv.at[j], den_send, den_rsem, same_ids[j]).start()

    pot_ref[core] = jnp.log(source_count * c_buf[1, 0])
    pot_ref[twin] = jnp.log(source_count * c_buf[1, 1])
    column.wait_send()
    mirror.wait_send()
    last = []
    for h in range(ROWS // SPAN):
        span = pl.ds(h * SPAN, SPAN)
        last.append(
            remote(
                num_t.at[pl.ds(0, TGT - 1), :, span], num_recv.at[:, :, span],
                num_send.at[h], num_rsem.at[h], twin_id,
            )
        )
    den_copy = remote(den_recv, den_recv, den_send, den_rsem, twin_id)
    den_copy.wait_recv()
    den_total = den_t[...]
    for j in range(TGT - 1):
        den_total = den_total + den_recv[j]
    for h in range(ROWS // SPAN):
        span = pl.ds(h * SPAN, SPAN)
        last[h].wait_recv()
        num_total = num_t[me_t, :, span]
        for j in range(TGT - 1):
            num_total = num_total + num_recv[j, :, span]
        map_ref[:, span] = num_total / den_total[:, h * SPAN : (h + 1) * SPAN]
    for copy in last + [den_copy]:
        copy.wait_send()


def finish(map_in, pot_in, map_out, pot_out, sem):
    copies = [
        pltpu.make_async_copy(map_in, map_out, sem.at[0]),
        pltpu.make_async_copy(pot_in, pot_out, sem.at[1]),
    ]
    for copy in copies:
        copy.start()
    for copy in copies:
        copy.wait()


def in_hbm(x):
    return pltpu.with_memory_space_constraint(x, pltpu.HBM)


def on_device(source_items, target_items, source_mass, target_mass):
    source_count = source_items.shape[0] * lax.axis_size("src")
    hbm_spec = any_spec = pl.BlockSpec(memory_space=pltpu.HBM)
    vmem_spec = pl.BlockSpec(memory_space=pltpu.VMEM)
    vmem, dma = pltpu.VMEM, pltpu.SemaphoreType.DMA
    mapped, potential = pl.pallas_call(
        functools.partial(kernel, float(source_count)),
        out_shape=(
            jax.ShapeDtypeStruct((SLIVER, ROWS), F32),
            jax.ShapeDtypeStruct((PAIR, TILES, LANES), F32),
        ),
        in_specs=[any_spec] * 4,
        out_specs=(vmem_spec, vmem_spec),
        scratch_shapes=[
            vmem((ROWS, EMBED), BF16),
            vmem((PAIR, HALF, 2 * EMBED), BF16),
            vmem((ROWS // LANES, LANES), F32),
            vmem((TILES, LANES), F32),
            vmem((PAIR, TILES, ROWS, LANES), F32),
            vmem((TILES, LANES), F32),
            vmem((2, TILES, LANES), F32),
            vmem((2, TILES, LANES), F32),
            vmem((2, RING, TILES, LANES), F32),
            vmem((2, DEPTH, TILES, LANES), F32),
            vmem((2, PAIR, TILES, LANES), F32),
            vmem((ROWS, LANES), F32),
            vmem((TGT, ROWS // LANES, LANES), F32),
            vmem((ROWS // LANES, LANES), F32),
            vmem((ROWS, LANES), F32),
            vmem((ROWS, 2 * EMBED), F32),
            vmem((TGT, SLIVER, ROWS), F32),
            vmem((TGT - 1, SLIVER, ROWS), F32),
            vmem((1, ROWS), F32),
            vmem((TGT - 1, 1, ROWS), F32),
            dma((7,)),
            pltpu.SemaphoreType.REGULAR,
            dma((2,)),
            dma((2,)),
            dma((2,)),
            dma((2,)),
            dma((2,)),
            dma((2,)),
            dma((2,)),
            dma((2,)),
            dma,
            dma,
            dma((ROWS // SPAN,)),
            dma((ROWS // SPAN,)),
            dma,
            dma,
        ],
        compiler_params=pltpu.CompilerParams(
            collective_id=0,
            has_side_effects=True,
            vmem_limit_bytes=LIMIT * 1024,
        ),
    )(
        in_hbm(source_items),
        in_hbm(target_items.reshape(PAIR, HALF, EMBED)),
        in_hbm(source_mass.reshape(ROWS // LANES, LANES)),
        in_hbm(target_mass.reshape(PAIR, TILES, LANES)),
    )
    mapped, potential = pl.pallas_call(
        finish,
        out_shape=(
            jax.ShapeDtypeStruct((SLIVER, ROWS), F32),
            jax.ShapeDtypeStruct((PAIR, TILES, LANES), F32),
        ),
        in_specs=[vmem_spec] * 2,
        out_specs=(hbm_spec, hbm_spec),
        scratch_shapes=[dma((2,))],
        compiler_params=pltpu.CompilerParams(vmem_limit_bytes=LIMIT * 1024),
    )(mapped, potential)
    return mapped.T, potential.reshape(COLS)


def solution(mesh):
    in_specs = (P("src", None), P("tgt", None), P("src"), P("tgt"))
    out_specs = (P("src", "tgt"), P("tgt"))
    return jax.shard_map(
        on_device, mesh=mesh, in_specs=in_specs, out_specs=out_specs, check_vma=False
    )
```

```python
import functools
import math

import jax
import jax.numpy as jnp
from jax import lax
from jax.experimental import pallas as pl
from jax.experimental.pallas import tpu as pltpu
from jax.sharding import PartitionSpec as P

ROWS = 512
COLS = 4096
EMBED = 128
RING = 4
DEPTH = 12
PAIR = 2
HALF = COLS // PAIR
LANES = 128
TILES = HALF // LANES
TGT = 8
SLIVER = EMBED // TGT
SPAN = 256
LIMIT = 40 * 1024
MESH = pl.DeviceIdType.MESH
F32 = jnp.float32
BF16 = jnp.bfloat16
RING_STEPS = (2, 1, 3)
DEPTH_STEPS = (6, 5, 7, 4, 8, 3, 9, 2, 10, 1, 11)
DEPTH_ORDER = (0, 1, 2, 3, 11, 4, 10, 5, 9, 6, 8, 7)
TGT_STEPS = ((2, 1), (2, 0), (1, 1), (3, 1), (1, 0), (3, 0), (0, 1))


def kernel(
    source_count,
    s_hbm, t_hbm, rmass_hbm, cmass_hbm,
    map_ref, pot_ref,
    s_v, text, rmass, cmass, kmat,
    part, cross_out, y_buf, z_buf, c_buf,
    row_acc, row_buf, row_scale, row_wide,
    num, num_t, num_recv, den_t, den_recv,
    load_sem, enter_sem, y_send, y_recv, z_send, z_recv,
    c_send, c_recv, row_send, row_recv, num_send, num_rsem, den_send, den_rsem,
):
    me_s, me_t = lax.axis_index("src"), lax.axis_index("tgt")
    core = lax.rem(me_s, PAIR)
    chip = lax.div(me_s, PAIR)
    zed = lax.rem(chip, DEPTH)
    ring = lax.div(chip, DEPTH)
    twin = 1 - core
    place_x, place_y = lax.div(me_t, 2), lax.rem(me_t, 2)

    def source(ring_at, zed_at, core_at):
        return (ring_at * DEPTH + zed_at) * PAIR + core_at

    twin_id = (source(ring, zed, twin), me_t)
    ring_ids = [(source(lax.rem(ring + k, RING), zed, core), me_t) for k in RING_STEPS]
    ring_cross_ids = [
        (source(lax.rem(ring + k, RING), zed, twin), me_t) for k in RING_STEPS
    ]
    berth = ring * PAIR + core
    depth_at = [lax.rem(zed + k, DEPTH) for k in DEPTH_STEPS]
    depth_ids = [(source(ring, there, core), me_t) for there in depth_at]
    tgt_at = [
        lax.rem(place_x + dx, 4) * 2 + lax.rem(place_y + dy, 2) for dx, dy in TGT_STEPS
    ]
    same_ids = [(me_s, there) for there in tgt_at]

    quarter = HALF // 2
    loads = [pltpu.make_async_copy(s_hbm, s_v, load_sem.at[0])]
    for i, (side, owner) in enumerate(((1, twin), (1, twin), (0, core), (0, core))):
        span = pl.ds(i % 2 * quarter, quarter)
        loads.append(
            pltpu.make_async_copy(
                t_hbm.at[owner, span, :],
                text.at[side, span, pl.ds(0, EMBED)],
                load_sem.at[i + 1],
            )
        )
    loads += [
        pltpu.make_async_copy(rmass_hbm, rmass, load_sem.at[5]),
        pltpu.make_async_copy(cmass_hbm.at[core], cmass, load_sem.at[6]),
    ]
    for load in loads:
        load.start()

    barrier = pltpu.get_barrier_semaphore()
    friends = ring_ids + ring_cross_ids + same_ids + [twin_id]
    for friend in friends:
        pl.semaphore_signal(barrier, inc=1, device_id=friend, device_id_type=MESH)
    for there, friend in zip(depth_at, depth_ids):

        @pl.when(there > zed)
        def _():
            pl.semaphore_signal(barrier, inc=1, device_id=friend, device_id_type=MESH)

    def remote(src, dst, send, recv, where):
        return pltpu.make_async_remote_copy(
            src_ref=src, dst_ref=dst, send_sem=send, recv_sem=recv,
            device_id=where, device_id_type=MESH,
        )

    log2e = 1.4426950408889634
    factor = 2.0 / math.sqrt(EMBED) * log2e
    block = 256

    def kernel_piece(side, piece, sums_ref):
        sums = None
        for m in range(ROWS // block):
            logits = lax.dot_general(
                s_v[pl.ds(m * block, block), :],
                text[side, pl.ds(piece * 256, 256), pl.ds(0, EMBED)],
                (((1,), (1,)), ((), ())), preferred_element_type=F32,
            )
            tile = jnp.exp2(logits * factor)
            for i in range(2):
                kmat[side, piece * 2 + i, pl.ds(m * block, block), :] = tile[
                    :, i * LANES : (i + 1) * LANES
                ]
            term = jnp.sum(tile.reshape(block // 8, 8, 256), axis=0)
            sums = term if sums is None else sums + term
        sums = jnp.sum(sums, axis=0, keepdims=True)
        for i in range(2):
            sums_ref[pl.ds(piece * 2 + i, 1), :] = sums[:, i * LANES : (i + 1) * LANES]

    def ring_start(it, same):
        src = y_buf.at[it, berth] if same else cross_out.at[it]
        for where in ring_ids if same else ring_cross_ids + [twin_id]:
            remote(
                src, y_buf.at[it, berth], y_send.at[it], y_recv.at[it], where
            ).start()

    loads[0].wait()
    pieces = HALF // 256
    for piece in range(pieces):
        if piece % (pieces // 2) == 0:
            loads[1 + piece // (pieces // 2)].wait()
        kernel_piece(1, piece, cross_out.at[0])
    for piece in range(pieces):
        if piece % (pieces // 2) == 0:
            loads[3 + piece // (pieces // 2)].wait()
        kernel_piece(0, piece, part)
    y_buf[0, berth] = part[...]
    pl.semaphore_wait(barrier, len(friends) + zed)
    ring_start(0, False)
    ring_start(0, True)
    for there, friend in zip(depth_at, depth_ids):

        @pl.when(there < zed)
        def _():
            pl.semaphore_signal(enter_sem, inc=1, device_id=friend, device_id_type=MESH)

    def finish_columns(it, meanwhile):
        meanwhile()
        others = pl.ds(0, PAIR * RING - 1)
        trio = remote(
            y_buf.at[it, others], y_buf.at[it, others],
            y_send.at[it], y_recv.at[it], twin_id,
        )
        trio.wait_recv()
        total = y_buf[it, 0]
        for k in range(1, PAIR * RING):
            total = total + y_buf[it, k]
        z_buf[it, zed] = total

        def send_depth(where):
            remote(
                z_buf.at[it, zed], z_buf.at[it, zed], z_send.at[it], z_recv.at[it], where
            ).start()

        if it == 0:
            for there, where in zip(depth_at, depth_ids):

                @pl.when(there < zed)
                def _():
                    send_depth(where)

            @pl.when(zed < DEPTH - 1)
            def _():
                pl.semaphore_wait(enter_sem, DEPTH - 1 - zed)

            for there, where in zip(depth_at, depth_ids):

                @pl.when(there > zed)
                def _():
                    send_depth(where)

        else:
            for there in DEPTH_ORDER:

                @pl.when(zed != there)
                def _():
                    send_depth((source(ring, there, core), me_t))

        trio.wait_send()
        others = pl.ds(0, DEPTH - 1)
        column = remote(
            z_buf.at[it, others], z_buf.at[it, others],
            z_send.at[it], z_recv.at[it], twin_id,
        )
        column.wait_recv()
        total = z_buf[it, 0]
        for k in range(1, DEPTH):
            total = total + z_buf[it, k]
        c_buf[it, 0] = cmass[...] / total
        mirror = remote(
            c_buf.at[it, 0], c_buf.at[it, 1], c_send.at[it], c_recv.at[it], twin_id
        )
        mirror.start()
        return column, mirror

    def first_wait():
        text[:, :, pl.ds(EMBED, EMBED)] = jnp.ones((PAIR, HALF, EMBED), BF16)
        for load in loads[5:]:
            load.wait()

    column, mirror = finish_columns(0, first_wait)

    step = 64
    for side in range(PAIR):
        if side == 1:
            column.wait_send()
            mirror.wait_recv()
        for b in range(ROWS // step):
            span = pl.ds(b * step, step)
            fold = kmat[side, 0, span, :] * c_buf[0, side, pl.ds(0, 1), :]
            for r in range(1, TILES):
                fold = fold + kmat[side, r, span, :] * c_buf[0, side, pl.ds(r, 1), :]
            if side == 1:
                fold = fold + row_acc[span, :]
            row_acc[span, :] = fold
    for i in range(ROWS // LANES):
        row_buf[me_t, pl.ds(i, 1), :] = jnp.sum(
            row_acc[pl.ds(i * LANES, LANES), :].T, axis=0, keepdims=True
        )
    for where in same_ids:
        remote(
            row_buf.at[me_t], row_buf.at[me_t], row_send, row_recv, where
        ).start()
    mirror.wait_send()
    rest = pl.ds(0, TGT - 1)
    rows = remote(row_buf.at[rest], row_buf.at[rest], row_send, row_recv, twin_id)
    rows.wait_recv()
    total = row_buf[0]
    for k in range(1, TGT):
        total = total + row_buf[k]
    row_scale[...] = rmass[...] / total
    for i in range(ROWS // LANES):
        wide = jnp.broadcast_to(row_scale[pl.ds(i, 1), :], (LANES, LANES))
        row_wide[pl.ds(i * LANES, LANES), :] = wide.T

    for side, sums_ref in ((1, cross_out.at[1]), (0, part)):
        sums = [jnp.zeros((8, LANES), F32)] * TILES
        for b in range(ROWS // step):
            span = pl.ds(b * step, step)
            wide = row_wide[span, :]
            for r in range(TILES):
                term = (kmat[side, r, span, :] * wide).reshape(step // 8, 8, LANES)
                sums[r] = sums[r] + jnp.sum(term, axis=0)
        for r in range(TILES):
            sums_ref[pl.ds(r, 1), :] = jnp.sum(sums[r], axis=0, keepdims=True)
        if side == 0:
            y_buf[1, berth] = part[...]
        ring_start(1, side == 0)

    column, mirror = finish_columns(1, rows.wait_send)

    def weighted(side, span):
        weights = jnp.concatenate(
            [
                (kmat[side, r, span, :] * c_buf[1, side, pl.ds(r, 1), :]).astype(BF16)
                for r in range(TILES)
            ],
            axis=1,
        )
        return jnp.dot(weights, text[side], preferred_element_type=F32)

    for h in range(ROWS // SPAN):
        span = pl.ds(h * SPAN, SPAN)
        num[span, :] = weighted(0, span)
    mirror.wait_recv()
    for h in range(ROWS // SPAN):
        span = pl.ds(h * SPAN, SPAN)
        term = weighted(1, span) + num[span, :]
        num_t[:, :, span] = term[:, :EMBED].T.reshape(TGT, SLIVER, SPAN)
        den_t[:, span] = term[:, EMBED:].T[:1]
        for j, there in enumerate(tgt_at):
            remote(
                num_t.at[there, :, span], num_recv.at[j, :, span],
                num_send.at[h], num_rsem.at[h], same_ids[j],
            ).start()
    for j in range(TGT - 1):
        remote(den_t, den_recv.at[j], den_send, den_rsem, same_ids[j]).start()

    pot_ref[core] = jnp.log(source_count * c_buf[1, 0])
    pot_ref[twin] = jnp.log(source_count * c_buf[1, 1])
    column.wait_send()
    mirror.wait_send()
    last = []
    for h in range(ROWS // SPAN):
        span = pl.ds(h * SPAN, SPAN)
        last.append(
            remote(
                num_t.at[pl.ds(0, TGT - 1), :, span], num_recv.at[:, :, span],
                num_send.at[h], num_rsem.at[h], twin_id,
            )
        )
    den_copy = remote(den_recv, den_recv, den_send, den_rsem, twin_id)
    den_copy.wait_recv()
    den_total = den_t[...]
    for j in range(TGT - 1):
        den_total = den_total + den_recv[j]
    for h in range(ROWS // SPAN):
        span = pl.ds(h * SPAN, SPAN)
        last[h].wait_recv()
        num_total = num_t[me_t, :, span]
        for j in range(TGT - 1):
            num_total = num_total + num_recv[j, :, span]
        map_ref[:, span] = num_total / den_total[:, h * SPAN : (h + 1) * SPAN]
    for copy in last + [den_copy]:
        copy.wait_send()


def finish(map_in, pot_in, map_out, pot_out, sem):
    copies = [
        pltpu.make_async_copy(map_in, map_out, sem.at[0]),
        pltpu.make_async_copy(pot_in, pot_out, sem.at[1]),
    ]
    for copy in copies:
        copy.start()
    for copy in copies:
        copy.wait()


def in_hbm(x):
    return pltpu.with_memory_space_constraint(x, pltpu.HBM)


def on_device(source_items, target_items, source_mass, target_mass):
    source_count = source_items.shape[0] * lax.axis_size("src")
    hbm_spec = any_spec = pl.BlockSpec(memory_space=pltpu.HBM)
    vmem_spec = pl.BlockSpec(memory_space=pltpu.VMEM)
    vmem, dma = pltpu.VMEM, pltpu.SemaphoreType.DMA
    mapped, potential = pl.pallas_call(
        functools.partial(kernel, float(source_count)),
        out_shape=(
            jax.ShapeDtypeStruct((SLIVER, ROWS), F32),
            jax.ShapeDtypeStruct((PAIR, TILES, LANES), F32),
        ),
        in_specs=[any_spec] * 4,
        out_specs=(vmem_spec, vmem_spec),
        scratch_shapes=[
            vmem((ROWS, EMBED), BF16),
            vmem((PAIR, HALF, 2 * EMBED), BF16),
            vmem((ROWS // LANES, LANES), F32),
            vmem((TILES, LANES), F32),
            vmem((PAIR, TILES, ROWS, LANES), F32),
            vmem((TILES, LANES), F32),
            vmem((2, TILES, LANES), F32),
            vmem((2, PAIR * RING, TILES, LANES), F32),
            vmem((2, DEPTH, TILES, LANES), F32),
            vmem((2, PAIR, TILES, LANES), F32),
            vmem((ROWS, LANES), F32),
            vmem((TGT, ROWS // LANES, LANES), F32),
            vmem((ROWS // LANES, LANES), F32),
            vmem((ROWS, LANES), F32),
            vmem((ROWS, 2 * EMBED), F32),
            vmem((TGT, SLIVER, ROWS), F32),
            vmem((TGT - 1, SLIVER, ROWS), F32),
            vmem((1, ROWS), F32),
            vmem((TGT - 1, 1, ROWS), F32),
            dma((7,)),
            pltpu.SemaphoreType.REGULAR,
            dma((2,)),
            dma((2,)),
            dma((2,)),
            dma((2,)),
            dma((2,)),
            dma((2,)),
            dma,
            dma,
            dma((ROWS // SPAN,)),
            dma((ROWS // SPAN,)),
            dma,
            dma,
        ],
        compiler_params=pltpu.CompilerParams(
            collective_id=0,
            has_side_effects=True,
            vmem_limit_bytes=LIMIT * 1024,
        ),
    )(
        in_hbm(source_items),
        in_hbm(target_items.reshape(PAIR, HALF, EMBED)),
        in_hbm(source_mass.reshape(ROWS // LANES, LANES)),
        in_hbm(target_mass.reshape(PAIR, TILES, LANES)),
    )
    mapped, potential = pl.pallas_call(
        finish,
        out_shape=(
            jax.ShapeDtypeStruct((SLIVER, ROWS), F32),
            jax.ShapeDtypeStruct((PAIR, TILES, LANES), F32),
        ),
        in_specs=[vmem_spec] * 2,
        out_specs=(hbm_spec, hbm_spec),
        scratch_shapes=[dma((2,))],
        compiler_params=pltpu.CompilerParams(vmem_limit_bytes=LIMIT * 1024),
    )(mapped, potential)
    return mapped.T, potential.reshape(COLS)


def solution(mesh):
    in_specs = (P("src", None), P("tgt", None), P("src"), P("tgt"))
    out_specs = (P("src", "tgt"), P("tgt"))
    return jax.shard_map(
        on_device, mesh=mesh, in_specs=in_specs, out_specs=out_specs, check_vma=False
    )
```

```python
import functools
import math

import jax
import jax.numpy as jnp
from jax import lax
from jax.experimental import pallas as pl
from jax.experimental.pallas import tpu as pltpu
from jax.sharding import PartitionSpec as P

ROWS = 512
COLS = 4096
EMBED = 128
RING = 4
DEPTH = 12
PAIR = 2
HALF = COLS // PAIR
LANES = 128
TILES = HALF // LANES
TGT = 8
SLIVER = EMBED // TGT
SPAN = 256
LIMIT = 40 * 1024
MESH = pl.DeviceIdType.MESH
F32 = jnp.float32
BF16 = jnp.bfloat16
RING_STEPS = (2, 1, 3)
DEPTH_STEPS = (6, 5, 7, 4, 8, 3, 9, 2, 10, 1, 11)
DEPTH_ORDER = (0, 1, 2, 3, 11, 4, 10, 5, 9, 6, 8, 7)
TGT_STEPS = ((2, 1), (2, 0), (1, 1), (3, 1), (1, 0), (3, 0), (0, 1))


def kernel(
    source_count,
    s_hbm, t_hbm, rmass_hbm, cmass_hbm,
    map_ref, pot_ref,
    s_v, text, rmass, cmass, kmat,
    part, cross_out, y_buf, z_buf, c_buf,
    row_acc, row_buf, row_scale, row_wide,
    num, num_t, num_recv, den_t, den_recv,
    load_sem, enter_sem, y_send, y_recv, z_send, z_recv,
    c_send, c_recv, row_send, row_recv, num_send, num_rsem, den_send, den_rsem,
):
    me_s, me_t = lax.axis_index("src"), lax.axis_index("tgt")
    core = lax.rem(me_s, PAIR)
    chip = lax.div(me_s, PAIR)
    zed = lax.rem(chip, DEPTH)
    ring = lax.div(chip, DEPTH)
    twin = 1 - core
    place_x, place_y = lax.div(me_t, 2), lax.rem(me_t, 2)

    def source(ring_at, zed_at, core_at):
        return (ring_at * DEPTH + zed_at) * PAIR + core_at

    twin_id = (source(ring, zed, twin), me_t)
    ring_ids = [(source(lax.rem(ring + k, RING), zed, core), me_t) for k in RING_STEPS]
    ring_cross_ids = [
        (source(lax.rem(ring + k, RING), zed, twin), me_t) for k in RING_STEPS
    ]
    berth = ring * PAIR + core
    depth_at = [lax.rem(zed + k, DEPTH) for k in DEPTH_STEPS]
    depth_ids = [(source(ring, there, core), me_t) for there in depth_at]
    tgt_at = [
        lax.rem(place_x + dx, 4) * 2 + lax.rem(place_y + dy, 2) for dx, dy in TGT_STEPS
    ]
    same_ids = [(me_s, there) for there in tgt_at]

    quarter = HALF // 2
    loads = [pltpu.make_async_copy(s_hbm, s_v, load_sem.at[0])]
    for i, (side, owner) in enumerate(((1, twin), (1, twin), (0, core), (0, core))):
        span = pl.ds(i % 2 * quarter, quarter)
        loads.append(
            pltpu.make_async_copy(
                t_hbm.at[owner, span, :],
                text.at[side, span, pl.ds(0, EMBED)],
                load_sem.at[i + 1],
            )
        )
    loads += [
        pltpu.make_async_copy(rmass_hbm, rmass, load_sem.at[5]),
        pltpu.make_async_copy(cmass_hbm.at[core], cmass, load_sem.at[6]),
    ]
    for load in loads:
        load.start()

    barrier = pltpu.get_barrier_semaphore()
    friends = ring_ids + ring_cross_ids + same_ids + [twin_id]
    for friend in friends:
        pl.semaphore_signal(barrier, inc=1, device_id=friend, device_id_type=MESH)
    for there, friend in zip(depth_at, depth_ids):

        @pl.when(there > zed)
        def _():
            pl.semaphore_signal(barrier, inc=1, device_id=friend, device_id_type=MESH)

    def remote(src, dst, send, recv, where):
        return pltpu.make_async_remote_copy(
            src_ref=src, dst_ref=dst, send_sem=send, recv_sem=recv,
            device_id=where, device_id_type=MESH,
        )

    log2e = 1.4426950408889634
    factor = 2.0 / math.sqrt(EMBED) * log2e
    block = 256

    def kernel_piece(side, piece, sums_ref):
        sums = None
        for m in range(ROWS // block):
            logits = lax.dot_general(
                s_v[pl.ds(m * block, block), :],
                text[side, pl.ds(piece * 256, 256), pl.ds(0, EMBED)],
                (((1,), (1,)), ((), ())), preferred_element_type=F32,
            )
            tile = jnp.exp2(logits * factor)
            for i in range(2):
                kmat[side, piece * 2 + i, pl.ds(m * block, block), :] = tile[
                    :, i * LANES : (i + 1) * LANES
                ]
            term = jnp.sum(tile.reshape(block // 8, 8, 256), axis=0)
            sums = term if sums is None else sums + term
        sums = jnp.sum(sums, axis=0, keepdims=True)
        for i in range(2):
            sums_ref[pl.ds(piece * 2 + i, 1), :] = sums[:, i * LANES : (i + 1) * LANES]

    def ring_start(it, same):
        src = y_buf.at[it, berth] if same else cross_out.at[it]
        for where in ring_ids if same else ring_cross_ids + [twin_id]:
            remote(
                src, y_buf.at[it, berth], y_send.at[it], y_recv.at[it], where
            ).start()

    loads[0].wait()
    pieces = HALF // 256
    for piece in range(pieces):
        if piece % (pieces // 2) == 0:
            loads[1 + piece // (pieces // 2)].wait()
        kernel_piece(1, piece, cross_out.at[0])
    for piece in range(pieces):
        if piece % (pieces // 2) == 0:
            loads[3 + piece // (pieces // 2)].wait()
        kernel_piece(0, piece, part)
    y_buf[0, berth] = part[...]
    pl.semaphore_wait(barrier, len(friends) + zed)
    ring_start(0, False)
    ring_start(0, True)
    for there, friend in zip(depth_at, depth_ids):

        @pl.when(there < zed)
        def _():
            pl.semaphore_signal(enter_sem, inc=1, device_id=friend, device_id_type=MESH)

    def finish_columns(it, meanwhile):
        meanwhile()
        others = pl.ds(0, PAIR * RING - 1)
        trio = remote(
            y_buf.at[it, others], y_buf.at[it, others],
            y_send.at[it], y_recv.at[it], twin_id,
        )
        trio.wait_recv()
        total = y_buf[it, 0]
        for k in range(1, PAIR * RING):
            total = total + y_buf[it, k]
        z_buf[it, zed] = total

        def send_depth(where):
            remote(
                z_buf.at[it, zed], z_buf.at[it, zed], z_send.at[it], z_recv.at[it], where
            ).start()

        if it == 0:
            for there, where in zip(depth_at, depth_ids):

                @pl.when(there < zed)
                def _():
                    send_depth(where)

            @pl.when(zed < DEPTH - 1)
            def _():
                pl.semaphore_wait(enter_sem, DEPTH - 1 - zed)

            for there, where in zip(depth_at, depth_ids):

                @pl.when(there > zed)
                def _():
                    send_depth(where)

        else:
            for there in DEPTH_ORDER:

                @pl.when(zed != there)
                def _():
                    send_depth((source(ring, there, core), me_t))

        trio.wait_send()
        others = pl.ds(0, DEPTH - 1)
        column = remote(
            z_buf.at[it, others], z_buf.at[it, others],
            z_send.at[it], z_recv.at[it], twin_id,
        )
        column.wait_recv()
        total = z_buf[it, 0]
        for k in range(1, DEPTH):
            total = total + z_buf[it, k]
        c_buf[it, 0] = cmass[...] / total
        mirror = remote(
            c_buf.at[it, 0], c_buf.at[it, 1], c_send.at[it], c_recv.at[it], twin_id
        )
        mirror.start()
        return column, mirror

    def first_wait():
        text[:, :, pl.ds(EMBED, EMBED)] = jnp.ones((PAIR, HALF, EMBED), BF16)
        for load in loads[5:]:
            load.wait()

    column, mirror = finish_columns(0, first_wait)

    step = 64
    for side in range(PAIR):
        if side == 1:
            column.wait_send()
            mirror.wait_recv()
        for b in range(ROWS // step):
            span = pl.ds(b * step, step)
            fold = kmat[side, 0, span, :] * c_buf[0, side, pl.ds(0, 1), :]
            for r in range(1, TILES):
                fold = fold + kmat[side, r, span, :] * c_buf[0, side, pl.ds(r, 1), :]
            if side == 1:
                fold = fold + row_acc[span, :]
            row_acc[span, :] = fold
    for i in range(ROWS // LANES):
        row_buf[me_t, pl.ds(i, 1), :] = jnp.sum(
            row_acc[pl.ds(i * LANES, LANES), :].T, axis=0, keepdims=True
        )
    for where in same_ids:
        remote(
            row_buf.at[me_t], row_buf.at[me_t], row_send, row_recv, where
        ).start()
    mirror.wait_send()
    rest = pl.ds(0, TGT - 1)
    rows = remote(row_buf.at[rest], row_buf.at[rest], row_send, row_recv, twin_id)
    rows.wait_recv()
    total = row_buf[0]
    for k in range(1, TGT):
        total = total + row_buf[k]
    row_scale[...] = rmass[...] / total
    for i in range(ROWS // LANES):
        wide = jnp.broadcast_to(row_scale[pl.ds(i, 1), :], (LANES, LANES))
        row_wide[pl.ds(i * LANES, LANES), :] = wide.T

    for side, sums_ref in ((1, cross_out.at[1]), (0, part)):
        sums = [jnp.zeros((8, LANES), F32)] * TILES
        for b in range(ROWS // step):
            span = pl.ds(b * step, step)
            wide = row_wide[span, :]
            for r in range(TILES):
                term = (kmat[side, r, span, :] * wide).reshape(step // 8, 8, LANES)
                sums[r] = sums[r] + jnp.sum(term, axis=0)
        for r in range(TILES):
            sums_ref[pl.ds(r, 1), :] = jnp.sum(sums[r], axis=0, keepdims=True)
        if side == 0:
            y_buf[1, berth] = part[...]
        ring_start(1, side == 0)

    column, mirror = finish_columns(1, rows.wait_send)

    def weighted(side, span):
        weights = jnp.concatenate(
            [
                (kmat[side, r, span, :] * c_buf[1, side, pl.ds(r, 1), :]).astype(BF16)
                for r in range(TILES)
            ],
            axis=1,
        )
        return jnp.dot(weights, text[side], preferred_element_type=F32)

    for h in range(ROWS // SPAN):
        span = pl.ds(h * SPAN, SPAN)
        num[span, :] = weighted(0, span)
    mirror.wait_recv()
    for h in range(ROWS // SPAN):
        span = pl.ds(h * SPAN, SPAN)
        term = weighted(1, span) + num[span, :]
        num_t[:, :, span] = term[:, :EMBED].T.reshape(TGT, SLIVER, SPAN)
        den_t[:, span] = term[:, EMBED:].T[:1]
        for j, there in enumerate(tgt_at):
            remote(
                num_t.at[there, :, span], num_recv.at[j, :, span],
                num_send.at[h], num_rsem.at[h], same_ids[j],
            ).start()
            if h == ROWS // SPAN - 1:
                remote(den_t, den_recv.at[j], den_send, den_rsem, same_ids[j]).start()

    pot_ref[core] = jnp.log(source_count * c_buf[1, 0])
    pot_ref[twin] = jnp.log(source_count * c_buf[1, 1])
    column.wait_send()
    mirror.wait_send()
    last = []
    for h in range(ROWS // SPAN):
        span = pl.ds(h * SPAN, SPAN)
        last.append(
            remote(
                num_t.at[pl.ds(0, TGT - 1), :, span], num_recv.at[:, :, span],
                num_send.at[h], num_rsem.at[h], twin_id,
            )
        )
    den_copy = remote(den_recv, den_recv, den_send, den_rsem, twin_id)
    den_copy.wait_recv()
    den_total = den_t[...]
    for j in range(TGT - 1):
        den_total = den_total + den_recv[j]
    for h in range(ROWS // SPAN):
        span = pl.ds(h * SPAN, SPAN)
        last[h].wait_recv()
        num_total = num_t[me_t, :, span]
        for j in range(TGT - 1):
            num_total = num_total + num_recv[j, :, span]
        map_ref[:, span] = num_total / den_total[:, h * SPAN : (h + 1) * SPAN]
    for copy in last + [den_copy]:
        copy.wait_send()


def finish(map_in, pot_in, map_out, pot_out, sem):
    copies = [
        pltpu.make_async_copy(map_in, map_out, sem.at[0]),
        pltpu.make_async_copy(pot_in, pot_out, sem.at[1]),
    ]
    for copy in copies:
        copy.start()
    for copy in copies:
        copy.wait()


def in_hbm(x):
    return pltpu.with_memory_space_constraint(x, pltpu.HBM)


def on_device(source_items, target_items, source_mass, target_mass):
    source_count = source_items.shape[0] * lax.axis_size("src")
    hbm_spec = any_spec = pl.BlockSpec(memory_space=pltpu.HBM)
    vmem_spec = pl.BlockSpec(memory_space=pltpu.VMEM)
    vmem, dma = pltpu.VMEM, pltpu.SemaphoreType.DMA
    mapped, potential = pl.pallas_call(
        functools.partial(kernel, float(source_count)),
        out_shape=(
            jax.ShapeDtypeStruct((SLIVER, ROWS), F32),
            jax.ShapeDtypeStruct((PAIR, TILES, LANES), F32),
        ),
        in_specs=[any_spec] * 4,
        out_specs=(vmem_spec, vmem_spec),
        scratch_shapes=[
            vmem((ROWS, EMBED), BF16),
            vmem((PAIR, HALF, 2 * EMBED), BF16),
            vmem((ROWS // LANES, LANES), F32),
            vmem((TILES, LANES), F32),
            vmem((PAIR, TILES, ROWS, LANES), F32),
            vmem((TILES, LANES), F32),
            vmem((2, TILES, LANES), F32),
            vmem((2, PAIR * RING, TILES, LANES), F32),
            vmem((2, DEPTH, TILES, LANES), F32),
            vmem((2, PAIR, TILES, LANES), F32),
            vmem((ROWS, LANES), F32),
            vmem((TGT, ROWS // LANES, LANES), F32),
            vmem((ROWS // LANES, LANES), F32),
            vmem((ROWS, LANES), F32),
            vmem((ROWS, 2 * EMBED), F32),
            vmem((TGT, SLIVER, ROWS), F32),
            vmem((TGT - 1, SLIVER, ROWS), F32),
            vmem((1, ROWS), F32),
            vmem((TGT - 1, 1, ROWS), F32),
            dma((7,)),
            pltpu.SemaphoreType.REGULAR,
            dma((2,)),
            dma((2,)),
            dma((2,)),
            dma((2,)),
            dma((2,)),
            dma((2,)),
            dma,
            dma,
            dma((ROWS // SPAN,)),
            dma((ROWS // SPAN,)),
            dma,
            dma,
        ],
        compiler_params=pltpu.CompilerParams(
            collective_id=0,
            has_side_effects=True,
            vmem_limit_bytes=LIMIT * 1024,
        ),
    )(
        in_hbm(source_items),
        in_hbm(target_items.reshape(PAIR, HALF, EMBED)),
        in_hbm(source_mass.reshape(ROWS // LANES, LANES)),
        in_hbm(target_mass.reshape(PAIR, TILES, LANES)),
    )
    mapped, potential = pl.pallas_call(
        finish,
        out_shape=(
            jax.ShapeDtypeStruct((SLIVER, ROWS), F32),
            jax.ShapeDtypeStruct((PAIR, TILES, LANES), F32),
        ),
        in_specs=[vmem_spec] * 2,
        out_specs=(hbm_spec, hbm_spec),
        scratch_shapes=[dma((2,))],
        compiler_params=pltpu.CompilerParams(vmem_limit_bytes=LIMIT * 1024),
    )(mapped, potential)
    return mapped.T, potential.reshape(COLS)


def solution(mesh):
    in_specs = (P("src", None), P("tgt", None), P("src"), P("tgt"))
    out_specs = (P("src", "tgt"), P("tgt"))
    return jax.shard_map(
        on_device, mesh=mesh, in_specs=in_specs, out_specs=out_specs, check_vma=False
    )
```

```python
import functools
import math

import jax
import jax.numpy as jnp
from jax import lax
from jax.experimental import pallas as pl
from jax.experimental.pallas import tpu as pltpu
from jax.sharding import PartitionSpec as P

ROWS = 512
COLS = 4096
EMBED = 128
RING = 4
DEPTH = 12
PAIR = 2
HALF = COLS // PAIR
LANES = 128
TILES = HALF // LANES
TGT = 8
SLIVER = EMBED // TGT
SPAN = 256
LIMIT = 40 * 1024
MESH = pl.DeviceIdType.MESH
F32 = jnp.float32
BF16 = jnp.bfloat16
RING_STEPS = (2, 1, 3)
DEPTH_STEPS = (6, 5, 7, 4, 8, 3, 9, 2, 10, 1, 11)
TGT_STEPS = ((2, 1), (2, 0), (1, 1), (3, 1), (1, 0), (3, 0), (0, 1))


def kernel(
    source_count,
    s_hbm, t_hbm, rmass_hbm, cmass_hbm,
    map_ref, pot_ref,
    s_v, text, rmass, cmass, kmat,
    part, cross_out, y_buf, z_buf, c_buf,
    row_acc, row_buf, row_scale, row_wide,
    num, num_t, num_recv, den_t, den_recv,
    load_sem, enter_sem, y_send, y_recv, z_send, z_recv,
    c_send, c_recv, row_send, row_recv, num_send, num_rsem, den_send, den_rsem,
):
    me_s, me_t = lax.axis_index("src"), lax.axis_index("tgt")
    core = lax.rem(me_s, PAIR)
    chip = lax.div(me_s, PAIR)
    zed = lax.rem(chip, DEPTH)
    ring = lax.div(chip, DEPTH)
    twin = 1 - core
    place_x, place_y = lax.div(me_t, 2), lax.rem(me_t, 2)

    def source(ring_at, zed_at, core_at):
        return (ring_at * DEPTH + zed_at) * PAIR + core_at

    twin_id = (source(ring, zed, twin), me_t)
    ring_ids = [(source(lax.rem(ring + k, RING), zed, core), me_t) for k in RING_STEPS]
    ring_cross_ids = [
        (source(lax.rem(ring + k, RING), zed, twin), me_t) for k in RING_STEPS
    ]
    berth = ring * PAIR + core
    depth_at = [lax.rem(zed + k, DEPTH) for k in DEPTH_STEPS]
    depth_ids = [(source(ring, there, core), me_t) for there in depth_at]
    tgt_at = [
        lax.rem(place_x + dx, 4) * 2 + lax.rem(place_y + dy, 2) for dx, dy in TGT_STEPS
    ]
    same_ids = [(me_s, there) for there in tgt_at]

    quarter = HALF // 2
    loads = [pltpu.make_async_copy(s_hbm, s_v, load_sem.at[0])]
    for i, (side, owner) in enumerate(((1, twin), (1, twin), (0, core), (0, core))):
        span = pl.ds(i % 2 * quarter, quarter)
        loads.append(
            pltpu.make_async_copy(
                t_hbm.at[owner, span, :],
                text.at[side, span, pl.ds(0, EMBED)],
                load_sem.at[i + 1],
            )
        )
    loads += [
        pltpu.make_async_copy(rmass_hbm, rmass, load_sem.at[5]),
        pltpu.make_async_copy(cmass_hbm.at[core], cmass, load_sem.at[6]),
    ]
    for load in loads:
        load.start()

    barrier = pltpu.get_barrier_semaphore()
    friends = ring_ids + ring_cross_ids + same_ids + [twin_id]
    for friend in friends:
        pl.semaphore_signal(barrier, inc=1, device_id=friend, device_id_type=MESH)
    for there, friend in zip(depth_at, depth_ids):

        @pl.when(there > zed)
        def _():
            pl.semaphore_signal(barrier, inc=1, device_id=friend, device_id_type=MESH)

    def remote(src, dst, send, recv, where):
        return pltpu.make_async_remote_copy(
            src_ref=src, dst_ref=dst, send_sem=send, recv_sem=recv,
            device_id=where, device_id_type=MESH,
        )

    log2e = 1.4426950408889634
    factor = 2.0 / math.sqrt(EMBED) * log2e
    block = 256

    def kernel_piece(side, piece, sums_ref):
        sums = None
        for m in range(ROWS // block):
            logits = lax.dot_general(
                s_v[pl.ds(m * block, block), :],
                text[side, pl.ds(piece * 256, 256), pl.ds(0, EMBED)],
                (((1,), (1,)), ((), ())), preferred_element_type=F32,
            )
            tile = jnp.exp2(logits * factor)
            for i in range(2):
                kmat[side, piece * 2 + i, pl.ds(m * block, block), :] = tile[
                    :, i * LANES : (i + 1) * LANES
                ]
            term = jnp.sum(tile.reshape(block // 8, 8, 256), axis=0)
            sums = term if sums is None else sums + term
        sums = jnp.sum(sums, axis=0, keepdims=True)
        for i in range(2):
            sums_ref[pl.ds(piece * 2 + i, 1), :] = sums[:, i * LANES : (i + 1) * LANES]

    def ring_send(it, same, where):
        src = y_buf.at[it, berth] if same else cross_out.at[it]
        remote(src, y_buf.at[it, berth], y_send.at[it], y_recv.at[it], where).start()

    loads[0].wait()
    pieces = HALF // 256
    for piece in range(pieces):
        if piece % (pieces // 2) == 0:
            loads[1 + piece // (pieces // 2)].wait()
        kernel_piece(1, piece, cross_out.at[0])
    for piece in range(pieces):
        if piece % (pieces // 2) == 0:
            loads[3 + piece // (pieces // 2)].wait()
        kernel_piece(0, piece, part)
    y_buf[0, berth] = part[...]
    pl.semaphore_wait(barrier, len(friends) + zed)
    for same_id, cross_id in zip(ring_ids, ring_cross_ids):
        ring_send(0, False, cross_id)
        ring_send(0, True, same_id)
    ring_send(0, False, twin_id)
    for there, friend in zip(depth_at, depth_ids):

        @pl.when(there < zed)
        def _():
            pl.semaphore_signal(enter_sem, inc=1, device_id=friend, device_id_type=MESH)

    def finish_columns(it, meanwhile):
        meanwhile()
        others = pl.ds(0, PAIR * RING - 1)
        trio = remote(
            y_buf.at[it, others], y_buf.at[it, others],
            y_send.at[it], y_recv.at[it], twin_id,
        )
        trio.wait_recv()
        total = y_buf[it, 0]
        for k in range(1, PAIR * RING):
            total = total + y_buf[it, k]
        z_buf[it, zed] = total

        def send_depth(where):
            remote(
                z_buf.at[it, zed], z_buf.at[it, zed], z_send.at[it], z_recv.at[it], where
            ).start()

        if it == 0:
            for there, where in zip(depth_at, depth_ids):

                @pl.when(there < zed)
                def _():
                    send_depth(where)

            @pl.when(zed < DEPTH - 1)
            def _():
                pl.semaphore_wait(enter_sem, DEPTH - 1 - zed)

            for there, where in zip(depth_at, depth_ids):

                @pl.when(there > zed)
                def _():
                    send_depth(where)

        else:
            for j in range(DEPTH - 1):
                there = jnp.where(zed <= j, j + 1, j)
                send_depth((source(ring, there, core), me_t))

        trio.wait_send()
        others = pl.ds(0, DEPTH - 1)
        column = remote(
            z_buf.at[it, others], z_buf.at[it, others],
            z_send.at[it], z_recv.at[it], twin_id,
        )
        column.wait_recv()
        total = z_buf[it, 0]
        for k in range(1, DEPTH):
            total = total + z_buf[it, k]
        c_buf[it, 0] = cmass[...] / total
        mirror = remote(
            c_buf.at[it, 0], c_buf.at[it, 1], c_send.at[it], c_recv.at[it], twin_id
        )
        mirror.start()
        return column, mirror

    def first_wait():
        text[:, :, pl.ds(EMBED, EMBED)] = jnp.ones((PAIR, HALF, EMBED), BF16)
        for load in loads[5:]:
            load.wait()

    column, mirror = finish_columns(0, first_wait)

    step = 64
    for side in range(PAIR):
        if side == 1:
            column.wait_send()
            mirror.wait_recv()
        for b in range(ROWS // step):
            span = pl.ds(b * step, step)
            fold = kmat[side, 0, span, :] * c_buf[0, side, pl.ds(0, 1), :]
            for r in range(1, TILES):
                fold = fold + kmat[side, r, span, :] * c_buf[0, side, pl.ds(r, 1), :]
            if side == 1:
                fold = fold + row_acc[span, :]
            row_acc[span, :] = fold
    for i in range(ROWS // LANES):
        row_buf[me_t, pl.ds(i, 1), :] = jnp.sum(
            row_acc[pl.ds(i * LANES, LANES), :].T, axis=0, keepdims=True
        )
    for where in same_ids:
        remote(
            row_buf.at[me_t], row_buf.at[me_t], row_send, row_recv, where
        ).start()
    mirror.wait_send()
    rest = pl.ds(0, TGT - 1)
    rows = remote(row_buf.at[rest], row_buf.at[rest], row_send, row_recv, twin_id)
    rows.wait_recv()
    total = row_buf[0]
    for k in range(1, TGT):
        total = total + row_buf[k]
    row_scale[...] = rmass[...] / total
    for i in range(ROWS // LANES):
        wide = jnp.broadcast_to(row_scale[pl.ds(i, 1), :], (LANES, LANES))
        row_wide[pl.ds(i * LANES, LANES), :] = wide.T

    for side, sums_ref in ((1, cross_out.at[1]), (0, part)):
        sums = [jnp.zeros((8, LANES), F32)] * TILES
        for b in range(ROWS // step):
            span = pl.ds(b * step, step)
            wide = row_wide[span, :]
            for r in range(TILES):
                term = (kmat[side, r, span, :] * wide).reshape(step // 8, 8, LANES)
                sums[r] = sums[r] + jnp.sum(term, axis=0)
        for r in range(TILES):
            sums_ref[pl.ds(r, 1), :] = jnp.sum(sums[r], axis=0, keepdims=True)
        if side == 0:
            y_buf[1, berth] = part[...]
        for where in ring_cross_ids + [twin_id] if side else ring_ids:
            ring_send(1, side == 0, where)

    column, mirror = finish_columns(1, rows.wait_send)

    def weighted(side, span):
        weights = jnp.concatenate(
            [
                (kmat[side, r, span, :] * c_buf[1, side, pl.ds(r, 1), :]).astype(BF16)
                for r in range(TILES)
            ],
            axis=1,
        )
        return jnp.dot(weights, text[side], preferred_element_type=F32)

    num[...] = weighted(0, pl.ds(0, ROWS))
    mirror.wait_recv()
    for h in range(ROWS // SPAN):
        span = pl.ds(h * SPAN, SPAN)
        term = weighted(1, span) + num[span, :]
        num_t[:, :, span] = term[:, :EMBED].T.reshape(TGT, SLIVER, SPAN)
        den_t[:, span] = term[:, EMBED:].T[:1]
        for j, there in enumerate(tgt_at):
            remote(
                num_t.at[there, :, span], num_recv.at[j, :, span],
                num_send.at[h], num_rsem.at[h], same_ids[j],
            ).start()
            if h == ROWS // SPAN - 1:
                remote(den_t, den_recv.at[j], den_send, den_rsem, same_ids[j]).start()

    pot_ref[core] = jnp.log(source_count * c_buf[1, 0])
    pot_ref[twin] = jnp.log(source_count * c_buf[1, 1])
    column.wait_send()
    mirror.wait_send()
    last = []
    for h in range(ROWS // SPAN):
        span = pl.ds(h * SPAN, SPAN)
        last.append(
            remote(
                num_t.at[pl.ds(0, TGT - 1), :, span], num_recv.at[:, :, span],
                num_send.at[h], num_rsem.at[h], twin_id,
            )
        )
    den_copy = remote(den_recv, den_recv, den_send, den_rsem, twin_id)
    totals = []
    for h in range(ROWS // SPAN):
        if h == ROWS // SPAN - 1:
            den_copy.wait_recv()
            den_total = den_t[...]
            for j in range(TGT - 1):
                den_total = den_total + den_recv[j]
        span = pl.ds(h * SPAN, SPAN)
        last[h].wait_recv()
        num_total = num_t[me_t, :, span]
        for j in range(TGT - 1):
            num_total = num_total + num_recv[j, :, span]
        totals.append(num_total)
    for h, num_total in enumerate(totals):
        span = pl.ds(h * SPAN, SPAN)
        map_ref[:, span] = num_total / den_total[:, h * SPAN : (h + 1) * SPAN]
    for copy in last + [den_copy]:
        copy.wait_send()


def finish(map_in, pot_in, map_out, pot_out, sem):
    copies = [
        pltpu.make_async_copy(map_in, map_out, sem.at[0]),
        pltpu.make_async_copy(pot_in, pot_out, sem.at[1]),
    ]
    for copy in copies:
        copy.start()
    for copy in copies:
        copy.wait()


def in_hbm(x):
    return pltpu.with_memory_space_constraint(x, pltpu.HBM)


def on_device(source_items, target_items, source_mass, target_mass):
    source_count = source_items.shape[0] * lax.axis_size("src")
    hbm_spec = any_spec = pl.BlockSpec(memory_space=pltpu.HBM)
    vmem_spec = pl.BlockSpec(memory_space=pltpu.VMEM)
    vmem, dma = pltpu.VMEM, pltpu.SemaphoreType.DMA
    mapped, potential = pl.pallas_call(
        functools.partial(kernel, float(source_count)),
        out_shape=(
            jax.ShapeDtypeStruct((SLIVER, ROWS), F32),
            jax.ShapeDtypeStruct((PAIR, TILES, LANES), F32),
        ),
        in_specs=[any_spec] * 4,
        out_specs=(vmem_spec, vmem_spec),
        scratch_shapes=[
            vmem((ROWS, EMBED), BF16),
            vmem((PAIR, HALF, 2 * EMBED), BF16),
            vmem((ROWS // LANES, LANES), F32),
            vmem((TILES, LANES), F32),
            vmem((PAIR, TILES, ROWS, LANES), F32),
            vmem((TILES, LANES), F32),
            vmem((2, TILES, LANES), F32),
            vmem((2, PAIR * RING, TILES, LANES), F32),
            vmem((2, DEPTH, TILES, LANES), F32),
            vmem((2, PAIR, TILES, LANES), F32),
            vmem((ROWS, LANES), F32),
            vmem((TGT, ROWS // LANES, LANES), F32),
            vmem((ROWS // LANES, LANES), F32),
            vmem((ROWS, LANES), F32),
            vmem((ROWS, 2 * EMBED), F32),
            vmem((TGT, SLIVER, ROWS), F32),
            vmem((TGT - 1, SLIVER, ROWS), F32),
            vmem((1, ROWS), F32),
            vmem((TGT - 1, 1, ROWS), F32),
            dma((7,)),
            pltpu.SemaphoreType.REGULAR,
            dma((2,)),
            dma((2,)),
            dma((2,)),
            dma((2,)),
            dma((2,)),
            dma((2,)),
            dma,
            dma,
            dma((ROWS // SPAN,)),
            dma((ROWS // SPAN,)),
            dma,
            dma,
        ],
        compiler_params=pltpu.CompilerParams(
            collective_id=0,
            has_side_effects=True,
            vmem_limit_bytes=LIMIT * 1024,
        ),
    )(
        in_hbm(source_items),
        in_hbm(target_items.reshape(PAIR, HALF, EMBED)),
        in_hbm(source_mass.reshape(ROWS // LANES, LANES)),
        in_hbm(target_mass.reshape(PAIR, TILES, LANES)),
    )
    mapped, potential = pl.pallas_call(
        finish,
        out_shape=(
            jax.ShapeDtypeStruct((SLIVER, ROWS), F32),
            jax.ShapeDtypeStruct((PAIR, TILES, LANES), F32),
        ),
        in_specs=[vmem_spec] * 2,
        out_specs=(hbm_spec, hbm_spec),
        scratch_shapes=[dma((2,))],
        compiler_params=pltpu.CompilerParams(vmem_limit_bytes=LIMIT * 1024),
    )(mapped, potential)
    return mapped.T, potential.reshape(COLS)


def solution(mesh):
    in_specs = (P("src", None), P("tgt", None), P("src"), P("tgt"))
    out_specs = (P("src", "tgt"), P("tgt"))
    return jax.shard_map(
        on_device, mesh=mesh, in_specs=in_specs, out_specs=out_specs, check_vma=False
    )
```

```python
import functools
import math

import jax
import jax.numpy as jnp
from jax import lax
from jax.experimental import pallas as pl
from jax.experimental.pallas import tpu as pltpu
from jax.sharding import PartitionSpec as P

ROWS = 512
COLS = 4096
EMBED = 128
RING = 4
DEPTH = 12
PAIR = 2
HALF = COLS // PAIR
LANES = 128
TILES = HALF // LANES
TGT = 8
SLIVER = EMBED // TGT
SPAN = 256
LIMIT = 40 * 1024
MESH = pl.DeviceIdType.MESH
F32 = jnp.float32
BF16 = jnp.bfloat16
RING_STEPS = (2, 1, 3)
DEPTH_STEPS = (6, 5, 7, 4, 8, 3, 9, 2, 10, 1, 11)
TGT_STEPS = ((2, 1), (2, 0), (1, 1), (3, 1), (1, 0), (3, 0), (0, 1))


def kernel(
    source_count,
    s_hbm, t_hbm, rmass_hbm, cmass_hbm,
    map_ref, pot_ref,
    s_v, text, rmass, cmass, kmat,
    part, cross_out, y_buf, z_buf, c_buf,
    row_acc, row_buf, row_scale, row_wide,
    num, num_t, num_recv, den_t, den_recv,
    load_sem, enter_sem, y_send, y_recv, z_send, z_recv,
    c_send, c_recv, row_send, row_recv, num_send, num_rsem, den_send, den_rsem,
):
    me_s, me_t = lax.axis_index("src"), lax.axis_index("tgt")
    core = lax.rem(me_s, PAIR)
    chip = lax.div(me_s, PAIR)
    zed = lax.rem(chip, DEPTH)
    ring = lax.div(chip, DEPTH)
    twin = 1 - core
    place_x, place_y = lax.div(me_t, 2), lax.rem(me_t, 2)

    def source(ring_at, zed_at, core_at):
        return (ring_at * DEPTH + zed_at) * PAIR + core_at

    twin_id = (source(ring, zed, twin), me_t)
    ring_ids = [(source(lax.rem(ring + k, RING), zed, core), me_t) for k in RING_STEPS]
    ring_cross_ids = [
        (source(lax.rem(ring + k, RING), zed, twin), me_t) for k in RING_STEPS
    ]
    berth = ring * PAIR + core
    depth_at = [lax.rem(zed + k, DEPTH) for k in DEPTH_STEPS]
    depth_ids = [(source(ring, there, core), me_t) for there in depth_at]
    tgt_at = [
        lax.rem(place_x + dx, 4) * 2 + lax.rem(place_y + dy, 2) for dx, dy in TGT_STEPS
    ]
    same_ids = [(me_s, there) for there in tgt_at]

    quarter = HALF // 2
    loads = [pltpu.make_async_copy(s_hbm, s_v, load_sem.at[0])]
    for i, (side, owner) in enumerate(((1, twin), (1, twin), (0, core), (0, core))):
        span = pl.ds(i % 2 * quarter, quarter)
        loads.append(
            pltpu.make_async_copy(
                t_hbm.at[owner, span, :],
                text.at[side, span, pl.ds(0, EMBED)],
                load_sem.at[i + 1],
            )
        )
    loads += [
        pltpu.make_async_copy(rmass_hbm, rmass, load_sem.at[5]),
        pltpu.make_async_copy(cmass_hbm.at[core], cmass, load_sem.at[6]),
    ]
    for load in loads:
        load.start()

    barrier = pltpu.get_barrier_semaphore()
    friends = ring_ids + ring_cross_ids + same_ids + [twin_id]
    for friend in friends:
        pl.semaphore_signal(barrier, inc=1, device_id=friend, device_id_type=MESH)
    for there, friend in zip(depth_at, depth_ids):

        @pl.when(there > zed)
        def _():
            pl.semaphore_signal(barrier, inc=1, device_id=friend, device_id_type=MESH)

    def remote(src, dst, send, recv, where):
        return pltpu.make_async_remote_copy(
            src_ref=src, dst_ref=dst, send_sem=send, recv_sem=recv,
            device_id=where, device_id_type=MESH,
        )

    log2e = 1.4426950408889634
    factor = 2.0 / math.sqrt(EMBED) * log2e
    block = 256

    def kernel_piece(side, piece, sums_ref):
        sums = None
        for m in range(ROWS // block):
            logits = lax.dot_general(
                s_v[pl.ds(m * block, block), :],
                text[side, pl.ds(piece * 256, 256), pl.ds(0, EMBED)],
                (((1,), (1,)), ((), ())), preferred_element_type=F32,
            )
            tile = jnp.exp2(logits * factor)
            for i in range(2):
                kmat[side, piece * 2 + i, pl.ds(m * block, block), :] = tile[
                    :, i * LANES : (i + 1) * LANES
                ]
            term = jnp.sum(tile.reshape(block // 8, 8, 256), axis=0)
            sums = term if sums is None else sums + term
        sums = jnp.sum(sums, axis=0, keepdims=True)
        for i in range(2):
            sums_ref[pl.ds(piece * 2 + i, 1), :] = sums[:, i * LANES : (i + 1) * LANES]

    def ring_send(it, same, where):
        src = y_buf.at[it, berth] if same else cross_out.at[it]
        remote(src, y_buf.at[it, berth], y_send.at[it], y_recv.at[it], where).start()

    loads[0].wait()
    pieces = HALF // 256
    for piece in range(pieces):
        if piece % (pieces // 2) == 0:
            loads[1 + piece // (pieces // 2)].wait()
        kernel_piece(1, piece, cross_out.at[0])
    for piece in range(pieces):
        if piece % (pieces // 2) == 0:
            loads[3 + piece // (pieces // 2)].wait()
        kernel_piece(0, piece, part)
    y_buf[0, berth] = part[...]
    pl.semaphore_wait(barrier, len(friends) + zed)
    for same_id, cross_id in zip(ring_ids, ring_cross_ids):
        ring_send(0, False, cross_id)
        ring_send(0, True, same_id)
    ring_send(0, False, twin_id)
    for there, friend in zip(depth_at, depth_ids):

        @pl.when(there < zed)
        def _():
            pl.semaphore_signal(enter_sem, inc=1, device_id=friend, device_id_type=MESH)

    def finish_columns(it, meanwhile):
        meanwhile()
        others = pl.ds(0, PAIR * RING - 1)
        trio = remote(
            y_buf.at[it, others], y_buf.at[it, others],
            y_send.at[it], y_recv.at[it], twin_id,
        )
        trio.wait_recv()
        total = y_buf[it, 0]
        for k in range(1, PAIR * RING):
            total = total + y_buf[it, k]
        z_buf[it, zed] = total

        def send_depth(where):
            remote(
                z_buf.at[it, zed], z_buf.at[it, zed], z_send.at[it], z_recv.at[it], where
            ).start()

        if it == 0:
            for there, where in zip(depth_at, depth_ids):

                @pl.when(there < zed)
                def _():
                    send_depth(where)

            @pl.when(zed < DEPTH - 1)
            def _():
                pl.semaphore_wait(enter_sem, DEPTH - 1 - zed)

            for there, where in zip(depth_at, depth_ids):

                @pl.when(there > zed)
                def _():
                    send_depth(where)

        else:
            for j in range(DEPTH - 1):
                there = jnp.where(zed <= j, j + 1, j)
                send_depth((source(ring, there, core), me_t))

        trio.wait_send()
        others = pl.ds(0, DEPTH - 1)
        column = remote(
            z_buf.at[it, others], z_buf.at[it, others],
            z_send.at[it], z_recv.at[it], twin_id,
        )
        column.wait_recv()
        total = z_buf[it, 0]
        for k in range(1, DEPTH):
            total = total + z_buf[it, k]
        c_buf[it, 0] = cmass[...] / total
        mirror = remote(
            c_buf.at[it, 0], c_buf.at[it, 1], c_send.at[it], c_recv.at[it], twin_id
        )
        mirror.start()
        return column, mirror

    def first_wait():
        text[:, :, pl.ds(EMBED, EMBED)] = jnp.ones((PAIR, HALF, EMBED), BF16)
        for load in loads[5:]:
            load.wait()

    column, mirror = finish_columns(0, first_wait)

    step = 128
    for side in range(PAIR):
        if side == 1:
            column.wait_send()
            mirror.wait_recv()
        for b in range(ROWS // step):
            span = pl.ds(b * step, step)
            fold = kmat[side, 0, span, :] * c_buf[0, side, pl.ds(0, 1), :]
            for r in range(1, TILES):
                fold = fold + kmat[side, r, span, :] * c_buf[0, side, pl.ds(r, 1), :]
            if side == 1:
                fold = fold + row_acc[span, :]
            row_acc[span, :] = fold
    for i in range(ROWS // LANES):
        row_buf[me_t, pl.ds(i, 1), :] = jnp.sum(
            row_acc[pl.ds(i * LANES, LANES), :].T, axis=0, keepdims=True
        )
    for where in same_ids:
        remote(
            row_buf.at[me_t], row_buf.at[me_t], row_send, row_recv, where
        ).start()
    mirror.wait_send()
    rest = pl.ds(0, TGT - 1)
    rows = remote(row_buf.at[rest], row_buf.at[rest], row_send, row_recv, twin_id)
    rows.wait_recv()
    total = row_buf[0]
    for k in range(1, TGT):
        total = total + row_buf[k]
    row_scale[...] = rmass[...] / total
    for i in range(ROWS // LANES):
        wide = jnp.broadcast_to(row_scale[pl.ds(i, 1), :], (LANES, LANES))
        row_wide[pl.ds(i * LANES, LANES), :] = wide.T

    for side, sums_ref in ((1, cross_out.at[1]), (0, part)):
        sums = [jnp.zeros((8, LANES), F32)] * TILES
        for b in range(ROWS // step):
            span = pl.ds(b * step, step)
            wide = row_wide[span, :]
            for r in range(TILES):
                term = (kmat[side, r, span, :] * wide).reshape(step // 8, 8, LANES)
                sums[r] = sums[r] + jnp.sum(term, axis=0)
        for r in range(TILES):
            sums_ref[pl.ds(r, 1), :] = jnp.sum(sums[r], axis=0, keepdims=True)
        if side == 0:
            y_buf[1, berth] = part[...]
        for where in ring_cross_ids + [twin_id] if side else ring_ids:
            ring_send(1, side == 0, where)

    column, mirror = finish_columns(1, rows.wait_send)

    def weighted(side, span):
        weights = jnp.concatenate(
            [
                (kmat[side, r, span, :] * c_buf[1, side, pl.ds(r, 1), :]).astype(BF16)
                for r in range(TILES)
            ],
            axis=1,
        )
        return jnp.dot(weights, text[side], preferred_element_type=F32)

    num[...] = weighted(0, pl.ds(0, ROWS))
    mirror.wait_recv()
    for h in range(ROWS // SPAN):
        span = pl.ds(h * SPAN, SPAN)
        term = weighted(1, span) + num[span, :]
        num_t[:, :, span] = term[:, :EMBED].T.reshape(TGT, SLIVER, SPAN)
        den_t[:, span] = term[:, EMBED:].T[:1]
        for j, there in enumerate(tgt_at):
            remote(
                num_t.at[there, :, span], num_recv.at[j, :, span],
                num_send.at[h], num_rsem.at[h], same_ids[j],
            ).start()
            if h == ROWS // SPAN - 1:
                remote(den_t, den_recv.at[j], den_send, den_rsem, same_ids[j]).start()

    pot_ref[core] = jnp.log(source_count * c_buf[1, 0])
    pot_ref[twin] = jnp.log(source_count * c_buf[1, 1])
    column.wait_send()
    mirror.wait_send()
    last = []
    for h in range(ROWS // SPAN):
        span = pl.ds(h * SPAN, SPAN)
        last.append(
            remote(
                num_t.at[pl.ds(0, TGT - 1), :, span], num_recv.at[:, :, span],
                num_send.at[h], num_rsem.at[h], twin_id,
            )
        )
    den_copy = remote(den_recv, den_recv, den_send, den_rsem, twin_id)
    totals = []
    for h in range(ROWS // SPAN):
        if h == ROWS // SPAN - 1:
            den_copy.wait_recv()
            den_total = den_t[...]
            for j in range(TGT - 1):
                den_total = den_total + den_recv[j]
        span = pl.ds(h * SPAN, SPAN)
        last[h].wait_recv()
        num_total = num_t[me_t, :, span]
        for j in range(TGT - 1):
            num_total = num_total + num_recv[j, :, span]
        totals.append(num_total)
    for h, num_total in enumerate(totals):
        span = pl.ds(h * SPAN, SPAN)
        map_ref[:, span] = num_total / den_total[:, h * SPAN : (h + 1) * SPAN]
    for copy in last + [den_copy]:
        copy.wait_send()


def finish(map_in, pot_in, map_out, pot_out, sem):
    copies = [
        pltpu.make_async_copy(map_in, map_out, sem.at[0]),
        pltpu.make_async_copy(pot_in, pot_out, sem.at[1]),
    ]
    for copy in copies:
        copy.start()
    for copy in copies:
        copy.wait()


def in_hbm(x):
    return pltpu.with_memory_space_constraint(x, pltpu.HBM)


def on_device(source_items, target_items, source_mass, target_mass):
    source_count = source_items.shape[0] * lax.axis_size("src")
    hbm_spec = any_spec = pl.BlockSpec(memory_space=pltpu.HBM)
    vmem_spec = pl.BlockSpec(memory_space=pltpu.VMEM)
    vmem, dma = pltpu.VMEM, pltpu.SemaphoreType.DMA
    mapped, potential = pl.pallas_call(
        functools.partial(kernel, float(source_count)),
        out_shape=(
            jax.ShapeDtypeStruct((SLIVER, ROWS), F32),
            jax.ShapeDtypeStruct((PAIR, TILES, LANES), F32),
        ),
        in_specs=[any_spec] * 4,
        out_specs=(vmem_spec, vmem_spec),
        scratch_shapes=[
            vmem((ROWS, EMBED), BF16),
            vmem((PAIR, HALF, 2 * EMBED), BF16),
            vmem((ROWS // LANES, LANES), F32),
            vmem((TILES, LANES), F32),
            vmem((PAIR, TILES, ROWS, LANES), F32),
            vmem((TILES, LANES), F32),
            vmem((2, TILES, LANES), F32),
            vmem((2, PAIR * RING, TILES, LANES), F32),
            vmem((2, DEPTH, TILES, LANES), F32),
            vmem((2, PAIR, TILES, LANES), F32),
            vmem((ROWS, LANES), F32),
            vmem((TGT, ROWS // LANES, LANES), F32),
            vmem((ROWS // LANES, LANES), F32),
            vmem((ROWS, LANES), F32),
            vmem((ROWS, 2 * EMBED), F32),
            vmem((TGT, SLIVER, ROWS), F32),
            vmem((TGT - 1, SLIVER, ROWS), F32),
            vmem((1, ROWS), F32),
            vmem((TGT - 1, 1, ROWS), F32),
            dma((7,)),
            pltpu.SemaphoreType.REGULAR,
            dma((2,)),
            dma((2,)),
            dma((2,)),
            dma((2,)),
            dma((2,)),
            dma((2,)),
            dma,
            dma,
            dma((ROWS // SPAN,)),
            dma((ROWS // SPAN,)),
            dma,
            dma,
        ],
        compiler_params=pltpu.CompilerParams(
            collective_id=0,
            has_side_effects=True,
            vmem_limit_bytes=LIMIT * 1024,
        ),
    )(
        in_hbm(source_items),
        in_hbm(target_items.reshape(PAIR, HALF, EMBED)),
        in_hbm(source_mass.reshape(ROWS // LANES, LANES)),
        in_hbm(target_mass.reshape(PAIR, TILES, LANES)),
    )
    mapped, potential = pl.pallas_call(
        finish,
        out_shape=(
            jax.ShapeDtypeStruct((SLIVER, ROWS), F32),
            jax.ShapeDtypeStruct((PAIR, TILES, LANES), F32),
        ),
        in_specs=[vmem_spec] * 2,
        out_specs=(hbm_spec, hbm_spec),
        scratch_shapes=[dma((2,))],
        compiler_params=pltpu.CompilerParams(vmem_limit_bytes=LIMIT * 1024),
    )(mapped, potential)
    return mapped.T, potential.reshape(COLS)


def solution(mesh):
    in_specs = (P("src", None), P("tgt", None), P("src"), P("tgt"))
    out_specs = (P("src", "tgt"), P("tgt"))
    return jax.shard_map(
        on_device, mesh=mesh, in_specs=in_specs, out_specs=out_specs, check_vma=False
    )
```

```python
import functools
import math

import jax
import jax.numpy as jnp
from jax import lax
from jax.experimental import pallas as pl
from jax.experimental.pallas import tpu as pltpu
from jax.sharding import PartitionSpec as P

ROWS = 512
COLS = 4096
EMBED = 128
RING = 4
DEPTH = 12
PAIR = 2
HALF = COLS // PAIR
LANES = 128
TILES = HALF // LANES
TGT = 8
SLIVER = EMBED // TGT
SPAN = 128
LIMIT = 40 * 1024
MESH = pl.DeviceIdType.MESH
F32 = jnp.float32
BF16 = jnp.bfloat16
RING_STEPS = (2, 1, 3)
DEPTH_STEPS = (6, 5, 7, 4, 8, 3, 9, 2, 10, 1, 11)
TGT_STEPS = ((2, 1), (2, 0), (1, 1), (3, 1), (1, 0), (3, 0), (0, 1))


def kernel(
    source_count,
    s_hbm, t_hbm, rmass_hbm, cmass_hbm,
    map_ref, pot_ref,
    s_v, text, rmass, cmass, kmat,
    part, cross_out, y_buf, z_buf, c_buf,
    row_acc, row_buf, row_scale, row_wide,
    num, num_t, num_recv, den_t, den_recv,
    load_sem, enter_sem, y_send, y_recv, z_send, z_recv,
    c_send, c_recv, row_send, row_recv, num_send, num_rsem, den_send, den_rsem,
):
    me_s, me_t = lax.axis_index("src"), lax.axis_index("tgt")
    core = lax.rem(me_s, PAIR)
    chip = lax.div(me_s, PAIR)
    zed = lax.rem(chip, DEPTH)
    ring = lax.div(chip, DEPTH)
    twin = 1 - core
    place_x, place_y = lax.div(me_t, 2), lax.rem(me_t, 2)

    def source(ring_at, zed_at, core_at):
        return (ring_at * DEPTH + zed_at) * PAIR + core_at

    twin_id = (source(ring, zed, twin), me_t)
    ring_ids = [(source(lax.rem(ring + k, RING), zed, core), me_t) for k in RING_STEPS]
    ring_cross_ids = [
        (source(lax.rem(ring + k, RING), zed, twin), me_t) for k in RING_STEPS
    ]
    berth = ring * PAIR + core
    depth_at = [lax.rem(zed + k, DEPTH) for k in DEPTH_STEPS]
    depth_ids = [(source(ring, there, core), me_t) for there in depth_at]
    tgt_at = [
        lax.rem(place_x + dx, 4) * 2 + lax.rem(place_y + dy, 2) for dx, dy in TGT_STEPS
    ]
    same_ids = [(me_s, there) for there in tgt_at]

    quarter = HALF // 2
    loads = [pltpu.make_async_copy(s_hbm, s_v, load_sem.at[0])]
    for i, (side, owner) in enumerate(((1, twin), (1, twin), (0, core), (0, core))):
        span = pl.ds(i % 2 * quarter, quarter)
        loads.append(
            pltpu.make_async_copy(
                t_hbm.at[owner, span, :],
                text.at[side, span, pl.ds(0, EMBED)],
                load_sem.at[i + 1],
            )
        )
    loads += [
        pltpu.make_async_copy(rmass_hbm, rmass, load_sem.at[5]),
        pltpu.make_async_copy(cmass_hbm.at[core], cmass, load_sem.at[6]),
    ]
    for load in loads:
        load.start()

    barrier = pltpu.get_barrier_semaphore()
    friends = ring_ids + ring_cross_ids + same_ids + [twin_id]
    for friend in friends:
        pl.semaphore_signal(barrier, inc=1, device_id=friend, device_id_type=MESH)
    for there, friend in zip(depth_at, depth_ids):

        @pl.when(there > zed)
        def _():
            pl.semaphore_signal(barrier, inc=1, device_id=friend, device_id_type=MESH)

    def remote(src, dst, send, recv, where):
        return pltpu.make_async_remote_copy(
            src_ref=src, dst_ref=dst, send_sem=send, recv_sem=recv,
            device_id=where, device_id_type=MESH,
        )

    log2e = 1.4426950408889634
    factor = 2.0 / math.sqrt(EMBED) * log2e
    block = 256

    def kernel_piece(side, piece, sums_ref):
        sums = None
        for m in range(ROWS // block):
            logits = lax.dot_general(
                s_v[pl.ds(m * block, block), :],
                text[side, pl.ds(piece * 256, 256), pl.ds(0, EMBED)],
                (((1,), (1,)), ((), ())), preferred_element_type=F32,
            )
            tile = jnp.exp2(logits * factor)
            for i in range(2):
                kmat[side, piece * 2 + i, pl.ds(m * block, block), :] = tile[
                    :, i * LANES : (i + 1) * LANES
                ]
            term = jnp.sum(tile.reshape(block // 8, 8, 256), axis=0)
            sums = term if sums is None else sums + term
        sums = jnp.sum(sums, axis=0, keepdims=True)
        for i in range(2):
            sums_ref[pl.ds(piece * 2 + i, 1), :] = sums[:, i * LANES : (i + 1) * LANES]

    def ring_send(it, same, where):
        src = y_buf.at[it, berth] if same else cross_out.at[it]
        remote(src, y_buf.at[it, berth], y_send.at[it], y_recv.at[it], where).start()

    loads[0].wait()
    pieces = HALF // 256
    for piece in range(pieces):
        if piece % (pieces // 2) == 0:
            loads[1 + piece // (pieces // 2)].wait()
        kernel_piece(1, piece, cross_out.at[0])
    for piece in range(pieces):
        if piece % (pieces // 2) == 0:
            loads[3 + piece // (pieces // 2)].wait()
        kernel_piece(0, piece, part)
    y_buf[0, berth] = part[...]
    pl.semaphore_wait(barrier, len(friends) + zed)
    for same_id, cross_id in zip(ring_ids, ring_cross_ids):
        ring_send(0, False, cross_id)
        ring_send(0, True, same_id)
    ring_send(0, False, twin_id)
    for there, friend in zip(depth_at, depth_ids):

        @pl.when(there < zed)
        def _():
            pl.semaphore_signal(enter_sem, inc=1, device_id=friend, device_id_type=MESH)

    def finish_columns(it, meanwhile):
        meanwhile()
        others = pl.ds(0, PAIR * RING - 1)
        trio = remote(
            y_buf.at[it, others], y_buf.at[it, others],
            y_send.at[it], y_recv.at[it], twin_id,
        )
        trio.wait_recv()
        total = y_buf[it, 0]
        for k in range(1, PAIR * RING):
            total = total + y_buf[it, k]
        z_buf[it, zed] = total

        def send_depth(where):
            remote(
                z_buf.at[it, zed], z_buf.at[it, zed], z_send.at[it], z_recv.at[it], where
            ).start()

        if it == 0:
            for there, where in zip(depth_at, depth_ids):

                @pl.when(there < zed)
                def _():
                    send_depth(where)

            @pl.when(zed < DEPTH - 1)
            def _():
                pl.semaphore_wait(enter_sem, DEPTH - 1 - zed)

            for there, where in zip(depth_at, depth_ids):

                @pl.when(there > zed)
                def _():
                    send_depth(where)

        else:
            for j in range(DEPTH - 1):
                there = jnp.where(zed <= j, j + 1, j)
                send_depth((source(ring, there, core), me_t))

        trio.wait_send()
        others = pl.ds(0, DEPTH - 1)
        column = remote(
            z_buf.at[it, others], z_buf.at[it, others],
            z_send.at[it], z_recv.at[it], twin_id,
        )
        column.wait_recv()
        total = z_buf[it, 0]
        for k in range(1, DEPTH):
            total = total + z_buf[it, k]
        c_buf[it, 0] = cmass[...] / total
        mirror = remote(
            c_buf.at[it, 0], c_buf.at[it, 1], c_send.at[it], c_recv.at[it], twin_id
        )
        mirror.start()
        return column, mirror

    def first_wait():
        text[:, :, pl.ds(EMBED, EMBED)] = jnp.ones((PAIR, HALF, EMBED), BF16)
        for load in loads[5:]:
            load.wait()

    column, mirror = finish_columns(0, first_wait)

    step = 64
    for side in range(PAIR):
        if side == 1:
            column.wait_send()
            mirror.wait_recv()
        for b in range(ROWS // step):
            span = pl.ds(b * step, step)
            fold = kmat[side, 0, span, :] * c_buf[0, side, pl.ds(0, 1), :]
            for r in range(1, TILES):
                fold = fold + kmat[side, r, span, :] * c_buf[0, side, pl.ds(r, 1), :]
            if side == 1:
                fold = fold + row_acc[span, :]
            row_acc[span, :] = fold
    for i in range(ROWS // LANES):
        row_buf[me_t, pl.ds(i, 1), :] = jnp.sum(
            row_acc[pl.ds(i * LANES, LANES), :].T, axis=0, keepdims=True
        )
    for where in same_ids:
        remote(
            row_buf.at[me_t], row_buf.at[me_t], row_send, row_recv, where
        ).start()
    mirror.wait_send()
    rest = pl.ds(0, TGT - 1)
    rows = remote(row_buf.at[rest], row_buf.at[rest], row_send, row_recv, twin_id)
    rows.wait_recv()
    total = row_buf[0]
    for k in range(1, TGT):
        total = total + row_buf[k]
    row_scale[...] = rmass[...] / total
    for i in range(ROWS // LANES):
        wide = jnp.broadcast_to(row_scale[pl.ds(i, 1), :], (LANES, LANES))
        row_wide[pl.ds(i * LANES, LANES), :] = wide.T

    for side, sums_ref in ((1, cross_out.at[1]), (0, part)):
        sums = [jnp.zeros((8, LANES), F32)] * TILES
        for b in range(ROWS // step):
            span = pl.ds(b * step, step)
            wide = row_wide[span, :]
            for r in range(TILES):
                term = (kmat[side, r, span, :] * wide).reshape(step // 8, 8, LANES)
                sums[r] = sums[r] + jnp.sum(term, axis=0)
        for r in range(TILES):
            sums_ref[pl.ds(r, 1), :] = jnp.sum(sums[r], axis=0, keepdims=True)
        if side == 0:
            y_buf[1, berth] = part[...]
        for where in ring_cross_ids + [twin_id] if side else ring_ids:
            ring_send(1, side == 0, where)

    column, mirror = finish_columns(1, rows.wait_send)

    def weighted(side, span):
        weights = jnp.concatenate(
            [
                (kmat[side, r, span, :] * c_buf[1, side, pl.ds(r, 1), :]).astype(BF16)
                for r in range(TILES)
            ],
            axis=1,
        )
        return jnp.dot(weights, text[side], preferred_element_type=F32)

    num[...] = weighted(0, pl.ds(0, ROWS))
    mirror.wait_recv()
    for h in range(ROWS // SPAN):
        span = pl.ds(h * SPAN, SPAN)
        term = weighted(1, span) + num[span, :]
        num_t[:, :, span] = term[:, :EMBED].T.reshape(TGT, SLIVER, SPAN)
        den_t[:, span] = term[:, EMBED:].T[:1]
        for j, there in enumerate(tgt_at):
            remote(
                num_t.at[there, :, span], num_recv.at[j, :, span],
                num_send.at[h], num_rsem.at[h], same_ids[j],
            ).start()
            if h == ROWS // SPAN - 1:
                remote(den_t, den_recv.at[j], den_send, den_rsem, same_ids[j]).start()

    pot_ref[core] = jnp.log(source_count * c_buf[1, 0])
    pot_ref[twin] = jnp.log(source_count * c_buf[1, 1])
    column.wait_send()
    mirror.wait_send()
    last = []
    for h in range(ROWS // SPAN):
        span = pl.ds(h * SPAN, SPAN)
        last.append(
            remote(
                num_t.at[pl.ds(0, TGT - 1), :, span], num_recv.at[:, :, span],
                num_send.at[h], num_rsem.at[h], twin_id,
            )
        )
    den_copy = remote(den_recv, den_recv, den_send, den_rsem, twin_id)
    totals = []
    for h in range(ROWS // SPAN):
        if h == ROWS // SPAN - 1:
            den_copy.wait_recv()
            den_total = den_t[...]
            for j in range(TGT - 1):
                den_total = den_total + den_recv[j]
        span = pl.ds(h * SPAN, SPAN)
        last[h].wait_recv()
        num_total = num_t[me_t, :, span]
        for j in range(TGT - 1):
            num_total = num_total + num_recv[j, :, span]
        totals.append(num_total)
    for h, num_total in enumerate(totals):
        span = pl.ds(h * SPAN, SPAN)
        map_ref[:, span] = num_total / den_total[:, h * SPAN : (h + 1) * SPAN]
    for copy in last + [den_copy]:
        copy.wait_send()


def finish(map_in, pot_in, map_out, pot_out, sem):
    copies = [
        pltpu.make_async_copy(map_in, map_out, sem.at[0]),
        pltpu.make_async_copy(pot_in, pot_out, sem.at[1]),
    ]
    for copy in copies:
        copy.start()
    for copy in copies:
        copy.wait()


def in_hbm(x):
    return pltpu.with_memory_space_constraint(x, pltpu.HBM)


def on_device(source_items, target_items, source_mass, target_mass):
    source_count = source_items.shape[0] * lax.axis_size("src")
    hbm_spec = any_spec = pl.BlockSpec(memory_space=pltpu.HBM)
    vmem_spec = pl.BlockSpec(memory_space=pltpu.VMEM)
    vmem, dma = pltpu.VMEM, pltpu.SemaphoreType.DMA
    mapped, potential = pl.pallas_call(
        functools.partial(kernel, float(source_count)),
        out_shape=(
            jax.ShapeDtypeStruct((SLIVER, ROWS), F32),
            jax.ShapeDtypeStruct((PAIR, TILES, LANES), F32),
        ),
        in_specs=[any_spec] * 4,
        out_specs=(vmem_spec, vmem_spec),
        scratch_shapes=[
            vmem((ROWS, EMBED), BF16),
            vmem((PAIR, HALF, 2 * EMBED), BF16),
            vmem((ROWS // LANES, LANES), F32),
            vmem((TILES, LANES), F32),
            vmem((PAIR, TILES, ROWS, LANES), F32),
            vmem((TILES, LANES), F32),
            vmem((2, TILES, LANES), F32),
            vmem((2, PAIR * RING, TILES, LANES), F32),
            vmem((2, DEPTH, TILES, LANES), F32),
            vmem((2, PAIR, TILES, LANES), F32),
            vmem((ROWS, LANES), F32),
            vmem((TGT, ROWS // LANES, LANES), F32),
            vmem((ROWS // LANES, LANES), F32),
            vmem((ROWS, LANES), F32),
            vmem((ROWS, 2 * EMBED), F32),
            vmem((TGT, SLIVER, ROWS), F32),
            vmem((TGT - 1, SLIVER, ROWS), F32),
            vmem((1, ROWS), F32),
            vmem((TGT - 1, 1, ROWS), F32),
            dma((7,)),
            pltpu.SemaphoreType.REGULAR,
            dma((2,)),
            dma((2,)),
            dma((2,)),
            dma((2,)),
            dma((2,)),
            dma((2,)),
            dma,
            dma,
            dma((ROWS // SPAN,)),
            dma((ROWS // SPAN,)),
            dma,
            dma,
        ],
        compiler_params=pltpu.CompilerParams(
            collective_id=0,
            has_side_effects=True,
            vmem_limit_bytes=LIMIT * 1024,
        ),
    )(
        in_hbm(source_items),
        in_hbm(target_items.reshape(PAIR, HALF, EMBED)),
        in_hbm(source_mass.reshape(ROWS // LANES, LANES)),
        in_hbm(target_mass.reshape(PAIR, TILES, LANES)),
    )
    mapped, potential = pl.pallas_call(
        finish,
        out_shape=(
            jax.ShapeDtypeStruct((SLIVER, ROWS), F32),
            jax.ShapeDtypeStruct((PAIR, TILES, LANES), F32),
        ),
        in_specs=[vmem_spec] * 2,
        out_specs=(hbm_spec, hbm_spec),
        scratch_shapes=[dma((2,))],
        compiler_params=pltpu.CompilerParams(vmem_limit_bytes=LIMIT * 1024),
    )(mapped, potential)
    return mapped.T, potential.reshape(COLS)


def solution(mesh):
    in_specs = (P("src", None), P("tgt", None), P("src"), P("tgt"))
    out_specs = (P("src", "tgt"), P("tgt"))
    return jax.shard_map(
        on_device, mesh=mesh, in_specs=in_specs, out_specs=out_specs, check_vma=False
    )
```
